32 devices in a mesh: dp: 4 (over z), ctx: 8 (over y, x, core).
Axes of the slice: x: 2, y: 2, z: 4, core: 2. Of those that a mesh axis runs over, the one named last changes fastest.
Arguments:
- normed_input: bfloat16 [4, 1024, 8192], P('dp', 'ctx'), may hold values from -6 to 6
- queries: bfloat16 [4, 1024, 1024], P('dp', 'ctx'), may hold values from -6 to 6
- keys_values: bfloat16 [4, 1024, 256], P('dp', 'ctx'), may hold values from -6 to 6
- grad_output: bfloat16 [4, 1024, 1024], P('dp', 'ctx'), may hold values from -6 to 6
- doc_lengths: int32 [4, 3], P('dp'), may hold values from 1 to 5, 8 in all within a row
Outputs:
- grad_queries: bfloat16 [4, 1024, 1024], P('dp', 'ctx')
- grad_keys_values: bfloat16 [4, 1024, 256], P('dp', 'ctx')
- grad_weights: float32 [8192, 1280], P(('ctx', 'dp'))
The draws below stay inside these ranges and needn't reach their ends.
Inputs may be any that keep to these rules, and one draw needn't show every extreme that they name: `doc_lengths`: the lengths of a window sum to 8 shards; in every window the longest document spans exactly 5 shards.
All inputs are finite; a program needn't handle non-finite values.
Results may differ from the reference program's by a relative error of at most 0.012.
Values may be sent and summed in bfloat16 or wider, within the bound.
No kernel may reach another device: no remote copies, remote signals or barrier semaphores. Data moves between devices by JAX's collectives and lax.ppermute only.
A program may use at most 64 MiB of HBM per device.

```python
import math
import jax
import jax.numpy as jnp
import numpy as np
from jax import lax

D = 8192
HEAD = 128
GROUP = 8
SHARD = 128
WIN = 1024
MAXDOC = 5
DOCS = 3
COLS = 1280
N_DP = 4
N_CTX = 8


def draw_queries(key, part):
    key = jax.random.fold_in(key, 7)
    sampled = jnp.clip(jax.random.normal(key, (N_DP, N_CTX, SHARD, GROUP * HEAD), jnp.float32), -5.5, 5.5)
    return sampled.reshape(N_DP, N_CTX * SHARD, GROUP * HEAD).astype(jnp.bfloat16)


def draw_keys_values(key, part):
    key = jax.random.fold_in(key, 13)
    sampled = jnp.clip(jax.random.normal(key, (N_DP, N_CTX, SHARD, 2 * HEAD), jnp.float32), -5.5, 5.5)
    return sampled.reshape(N_DP, N_CTX * SHARD, 2 * HEAD).astype(jnp.bfloat16)


def raised(values, key, source, target, blocks, factor):
    owner, partner = [(jnp.arange(values.shape[axis_at]) // (values.shape[axis_at] // blocks)).reshape([-1 if axis == axis_at else 1 for axis in range(values.ndim)]) for axis_at in (source, target)]
    chosen = jax.random.permutation(key, blocks)[partner]
    strong = (owner == chosen) | (owner == (partner + blocks // 2) % blocks)
    return jnp.where(strong, factor * values, values)


def steps_of(own_key, dims, cuts, low, high):
    def one(axis_at, shards_of):
        draws = jax.random.uniform(jax.random.fold_in(jax.random.fold_in(own_key, 6), axis_at), (shards_of,), jnp.float32, low / len(cuts), high / len(cuts))
        return jnp.repeat(jnp.exp(draws), dims[axis_at] // shards_of).reshape((-1,) + (1,) * (len(dims) - axis_at - 1))

    level = one(*cuts[0])
    for cut in cuts[1:]:
        level = level * one(*cut)
    return level


def length_profile(amount, total, reach, lean):
    loads = [(1 << 20) // math.isqrt(standing ** lean) + 1 for standing in range(2, amount + 1)]
    spare, holding = total - reach - (amount - 1), [1] * (amount - 1)
    while spare > 0:
        movable = [i for i in range(amount - 1) if holding[i] < reach]
        pool, remaining = sum([loads[i] for i in movable]), spare
        for i in movable:
            extra = min(reach - holding[i], max(1, remaining * loads[i] // pool), spare)
            holding[i] = holding[i] + extra
            spare = spare - extra
    return np.array([reach] + holding)


def uneven_parts(key, amount, total, most, lean):
    if amount == 2:
        one = jax.random.randint(key, (), max(1, total - most), min(most, total - 1) + 1)
        return jnp.stack([one, total - one])
    tallies = jnp.asarray(length_profile(amount, total, most, lean), jnp.int32)
    couples = (amount - 1) // 2
    source_of, taker = tallies[1:1 + 2 * couples:2], tallies[2:2 + 2 * couples:2]
    slack = jnp.minimum(source_of - 1, most - taker)
    passed = jax.random.randint(jax.random.fold_in(key, 1), (couples,), 0, 1 << 20) % (slack + 1)
    tallies = tallies.at[1:1 + 2 * couples:2].set(source_of - passed).at[2:2 + 2 * couples:2].set(taker + passed)
    return tallies[jax.random.permutation(jax.random.fold_in(key, 2), amount)]


def noise(own_key, dims, deviation, bound, cuts=(), held_as=jnp.bfloat16):
    loudness = steps_of(own_key, dims, cuts, -0.22, 0.18) if cuts else 1.0
    values = jax.random.normal(own_key, dims, jnp.float32) * deviation * loudness
    return jnp.minimum(jnp.maximum(values, -bound), bound).astype(held_as)


def heavy_noise(stream_key, dims, deviation, limit, cuts, heavy, kind=jnp.bfloat16):
    drawn = deviation * jax.random.normal(stream_key, dims, jnp.float32)
    if cuts:
        drawn = drawn * steps_of(stream_key, dims, cuts, -0.22, 0.18)
    return jnp.clip(raised(drawn, jax.random.fold_in(stream_key, 3), *heavy), -limit, limit).astype(kind)


def setup_inputs(seed: int = 0) -> dict:
    key_of = jax.random.split(jax.random.key(seed), 6)
    return {
        "normed_input": heavy_noise(key_of[0], (N_DP, WIN, D), 1.0, 6.0, ((0, 4), (1, 8)), (0, 2, 4, 2.0)),
        "queries": draw_queries(jax.random.fold_in(key_of[5], 71), 0),
        "keys_values": draw_keys_values(jax.random.fold_in(key_of[5], 71), 0),
        "grad_output": noise(key_of[3], (N_DP, WIN, GROUP * HEAD), 1.0, 6.0, ((0, 4), (1, 8))),
        "doc_lengths": jax.vmap(lambda own: uneven_parts(own, DOCS, N_CTX, MAXDOC, 2))(jax.random.split(key_of[4], N_DP)).reshape((N_DP, DOCS)).astype(jnp.int32),
    }


def shard_firsts(doc_lens, count):
    doc_ends = jnp.cumsum(doc_lens).astype(jnp.int32)
    doc_starts = (doc_ends - doc_lens).astype(jnp.int32)
    shard_ids = jnp.arange(count, dtype=jnp.int32)
    picked = jnp.where(doc_starts[None, :] <= shard_ids[:, None], doc_starts[None, :], 0)
    return jnp.max(picked, axis=1).astype(jnp.int32)


def window_grads(win_q, win_kv, win_dout, win_lens):
    length = win_q.shape[0]
    first_shard = shard_firsts(win_lens, N_CTX)
    position = jnp.arange(length, dtype=jnp.int32)
    row_first = first_shard[position // SHARD]
    allowed = ((position[None, :] // SHARD) >= row_first[:, None]) & (position[None, :] <= position[:, None])
    softmax_scale = HEAD ** -0.5
    query_heads = win_q.reshape(length, GROUP, HEAD).astype(jnp.float32)
    key_rows = win_kv[:, :HEAD].astype(jnp.float32)
    value_rows = win_kv[:, HEAD:].astype(jnp.float32)
    grad_heads = win_dout.reshape(length, GROUP, HEAD).astype(jnp.float32)
    scores = jnp.einsum("sgh,kh->gsk", query_heads, key_rows) * softmax_scale
    masked = jnp.where(allowed[None], scores, -1e30)
    row_max = jnp.max(masked, axis=-1, keepdims=True)
    exps_kept = jnp.where(allowed[None], jnp.exp(masked - row_max), 0.0)
    probs = exps_kept / jnp.sum(exps_kept, axis=-1, keepdims=True)
    weights_wide = lax.optimization_barrier(probs.astype(jnp.bfloat16)).astype(jnp.float32)
    attended = jnp.einsum("gsk,kh->gsh", weights_wide, value_rows)
    row_dots = jnp.sum(jnp.transpose(grad_heads, (1, 0, 2)) * attended, axis=-1)
    dprobs = jnp.einsum("sgh,kh->gsk", grad_heads, value_rows)
    dscores = probs * (dprobs - row_dots[..., None])
    dscore_wide = lax.optimization_barrier(dscores.astype(jnp.bfloat16)).astype(jnp.float32)
    grad_query = (jnp.einsum("gsk,kh->sgh", dscore_wide, key_rows) * softmax_scale).astype(jnp.bfloat16)
    dscore_split = dscore_wide.reshape(GROUP, N_CTX, SHARD, length)
    weight_split = weights_wide.reshape(GROUP, N_CTX, SHARD, length)
    query_split = query_heads.reshape(N_CTX, SHARD, GROUP, HEAD)
    grad_split = grad_heads.reshape(N_CTX, SHARD, GROUP, HEAD)
    key_terms = jnp.einsum("gtsk,tsgh->tkh", dscore_split, query_split) * softmax_scale
    value_terms = jnp.einsum("gtsk,tsgh->tkh", weight_split, grad_split)
    kv_terms = jnp.concatenate([key_terms, value_terms], axis=2)
    kv_terms = lax.optimization_barrier(kv_terms.astype(jnp.bfloat16)).astype(jnp.float32)
    grad_kv = jnp.sum(kv_terms, axis=0).astype(jnp.bfloat16)
    return grad_query.reshape(length, GROUP * HEAD), grad_kv


def reference(normed_input, queries, keys_values, grad_output, doc_lengths):
    def window_step(running, window_items):
        win_x, win_q, win_kv, win_dout, win_lens = window_items
        grad_query, grad_kv = window_grads(win_q, win_kv, win_dout, win_lens)
        grad_cols = jnp.concatenate([grad_query, grad_kv], axis=1).astype(jnp.float32)
        running = running + jnp.dot(win_x.astype(jnp.float32).T, grad_cols, precision=lax.Precision.HIGHEST)
        return running, (grad_query, grad_kv)

    start_sum = jnp.zeros((D, COLS), jnp.float32)
    running, (grad_queries, grad_keys_values) = lax.scan(window_step, start_sum, (normed_input, queries, keys_values, grad_output, doc_lengths))
    return grad_queries, grad_keys_values, running
```

```python
import functools

import jax
import jax.numpy as jnp
from jax import lax
from jax.experimental import pallas as pl
from jax.experimental.pallas import tpu as pltpu
from jax.sharding import PartitionSpec as P

F32 = jnp.float32
BF16 = jnp.bfloat16
VMEM_LIMIT = 48 * 1024 * 1024


def dot(a, b, ca, cb):
    return lax.dot_general(a, b, (((ca,), (cb,)), ((), ())), preferred_element_type=F32)


def attention_kernel(own_ref, lens_ref, q_ref, do_ref, *refs, span, head, group, docs):
    kv_refs, (gq_ref, terms_ref) = refs[:span], refs[span:]
    rows = q_ref.shape[0]
    scale = head ** (-0.5)
    own = own_ref[0]
    first = jnp.int32(0)
    start = jnp.int32(0)
    for d in range(docs):
        first = jnp.where(start <= own, jnp.maximum(first, start), first)
        start = start + lens_ref[0, d]
    kv = jnp.concatenate([r[...] for r in kv_refs], axis=0)
    keys, values = kv[:, :head], kv[:, head:]
    keys_t = keys.T
    width = 2 * rows
    key_at = lax.broadcasted_iota(jnp.int32, (span * rows, width), 0)
    query_at = lax.broadcasted_iota(jnp.int32, (span * rows, width), 1) % rows
    low = (first - own + span - 1) * rows
    allowed = (key_at >= low) & (key_at <= query_at + (span - 1) * rows)
    dk = jnp.zeros((span * rows, head), F32)
    dv = jnp.zeros((span * rows, head), F32)
    for pair in range(group // 2):
        at = [2 * pair * head, (2 * pair + 1) * head]
        q2 = jnp.concatenate([q_ref[:, a : a + head] for a in at], axis=0)
        do2 = jnp.concatenate([do_ref[:, a : a + head] for a in at], axis=0)
        scores = jnp.where(allowed, dot(keys, q2, 1, 1) * scale, -1e30)
        exps = jnp.exp(scores - jnp.max(scores, axis=0, keepdims=True))
        probs = exps * (1.0 / jnp.sum(exps, axis=0, keepdims=True))
        probs_half = probs.astype(BF16)
        dprobs = dot(values, do2, 1, 1)
        row_dots = jnp.sum(probs_half.astype(F32) * dprobs, axis=0, keepdims=True)
        dscores_half = (probs * (dprobs - row_dots)).astype(BF16)
        dk = dk + dot(dscores_half, q2, 1, 0)
        dv = dv + dot(probs_half, do2, 1, 0)
        gq_t = dot(keys_t, dscores_half, 1, 0) * scale
        for i, a in enumerate(at):
            gq_ref[:, a : a + head] = gq_t[:, i * rows : (i + 1) * rows].T.astype(BF16)
    terms_ref[:, :, :head] = (dk * scale).astype(BF16).reshape(span, rows, head)
    terms_ref[:, :, head:] = dv.astype(BF16).reshape(span, rows, head)


def attention(own, lens, q, do, slots, head):
    span, rows = len(slots), q.shape[0]
    group = q.shape[1] // head
    smem = pl.BlockSpec(memory_space=pltpu.SMEM)
    vmem = pl.BlockSpec(memory_space=pltpu.VMEM)
    return pl.pallas_call(
        functools.partial(
            attention_kernel, span=span, head=head, group=group, docs=lens.shape[1]
        ),
        out_shape=(
            jax.ShapeDtypeStruct(q.shape, BF16),
            jax.ShapeDtypeStruct((span, rows, 2 * head), BF16),
        ),
        in_specs=[smem, smem] + [vmem] * (2 + span),
        out_specs=(vmem, vmem),
        compiler_params=pltpu.CompilerParams(vmem_limit_bytes=VMEM_LIMIT),
        cost_estimate=pl.CostEstimate(
            flops=12 * group * rows * rows * span * head,
            bytes_accessed=6 * q.size + 4 * span * rows * 2 * head,
            transcendentals=group * rows * rows * span,
        ),
        name="attention",
    )(own, lens, q, do, *slots)


def spread_kernel(place_ref, x_ref, *refs, ctx, dp, part):
    outs, sem = refs[:-1], refs[-1]
    z, c = place_ref[0], place_ref[1]
    core = c % 2
    first = 2 + 2 * core
    chips = (0, first, 6 - first, 6)
    copies = []
    for far in range(2):
        for at, flip in enumerate(chips):
            for other in range(2):
                dest = c ^ flip ^ other
                for high in range(2):
                    plane = 2 * high + (z % 2) ^ far
                    src = pl.multiple_of((dest * dp + plane) * part, part)
                    copies.append(
                        pltpu.make_async_copy(
                            x_ref.at[:, pl.ds(src, part)],
                            outs[4 * far + at].at[other, :, pl.ds(high * part, part)],
                            sem.at[len(copies)],
                        )
                    )
    for copy in copies:
        copy.start()
    for copy in copies:
        copy.wait()


def spread(place, x, ctx, dp):
    rows, width = x.shape
    part = width // (ctx * dp)
    piece = jax.ShapeDtypeStruct((2, rows, 2 * part), BF16)
    hbm = pl.BlockSpec(memory_space=pl.ANY)
    return pl.pallas_call(
        functools.partial(spread_kernel, ctx=ctx, dp=dp, part=part),
        out_shape=(piece,) * 8,
        in_specs=[pl.BlockSpec(memory_space=pltpu.SMEM), hbm],
        out_specs=(hbm,) * 8,
        scratch_shapes=[pltpu.SemaphoreType.DMA((32,))],
        cost_estimate=pl.CostEstimate(flops=0, bytes_accessed=4 * x.size, transcendentals=0),
        name="spread",
    )(place, x)


def turn_kernel(*refs):
    kept, siblings, out = refs[:8], refs[8:10], refs[10]
    rows = kept[0].shape[1]
    for at in range(4):
        for far in range(2):
            j = 2 * at + far
            out[:, j * rows : (j + 1) * rows] = kept[4 * far + at][0].T
            out[:, (8 + j) * rows : (9 + j) * rows] = siblings[far][at].T


def turn(kept, siblings):
    _, rows, width = kept[0].shape
    vmem = pl.BlockSpec(memory_space=pltpu.VMEM)
    half = pl.BlockSpec((1, rows, width), lambda i: (0, 0, 0))
    whole = pl.BlockSpec((4, rows, width), lambda i: (0, 0, 0))
    return pl.pallas_call(
        turn_kernel,
        grid=(1,),
        out_shape=jax.ShapeDtypeStruct((width, 16 * rows), BF16),
        in_specs=[half] * 8 + [whole] * 2,
        out_specs=pl.BlockSpec((width, 16 * rows), lambda i: (0, 0)),
        compiler_params=pltpu.CompilerParams(vmem_limit_bytes=VMEM_LIMIT),
        cost_estimate=pl.CostEstimate(
            flops=0, bytes_accessed=64 * rows * width, transcendentals=0
        ),
        name="turn",
    )(*kept, *siblings)


def fold_kernel(side_ref, x_ref, *refs):
    cols, out = refs[:-1], refs[-1]
    depth = cols[0].shape[0] * cols[0].shape[1]
    total = None
    for j, col in enumerate(cols):
        block = col[...].reshape(depth, col.shape[2])
        term = dot(x_ref[:, j * depth : (j + 1) * depth], block, 1, 0)
        total = term if total is None else total + term
    out[...] = total.astype(out.dtype)


def fold(side, turned, cols, dtype):
    width, depth = turned.shape
    half = width // 2
    n = cols[0].shape[2]
    return pl.pallas_call(
        fold_kernel,
        grid_spec=pltpu.PrefetchScalarGridSpec(
            num_scalar_prefetch=1,
            grid=(1,),
            in_specs=[pl.BlockSpec((half, depth), lambda i, side: (side[0], 0))]
            + [pl.BlockSpec(c.shape, lambda i, side: (0, 0, 0)) for c in cols],
            out_specs=pl.BlockSpec((half, n), lambda i, side: (0, 0)),
        ),
        out_shape=jax.ShapeDtypeStruct((half, n), dtype),
        compiler_params=pltpu.CompilerParams(vmem_limit_bytes=VMEM_LIMIT),
        cost_estimate=pl.CostEstimate(
            flops=2 * half * depth * n,
            bytes_accessed=2 * half * depth + 2 * depth * n + 4 * half * n,
            transcendentals=0,
        ),
        name="fold",
    )(side, turned, *cols)


def fold_rows(features, piece_rows):
    return lax.dot_general(
        features, piece_rows, (((0,), (0,)), ((), ())), preferred_element_type=F32
    )


def attend(own_index, queries, keys_values, grad_output, doc_lengths):
    ctx = lax.axis_size("ctx")
    span = ctx // 2 + 1
    own_kv = keys_values[0]
    slots = [own_kv]
    for d in range(1, span):
        moved = lax.ppermute(own_kv, "ctx", [(i, (i + d) % ctx) for i in range(ctx)])
        slots.insert(0, moved)
    head = keys_values.shape[2] // 2
    return attention(
        own_index[None], doc_lengths, queries[0], grad_output[0], slots, head
    )


def sum_terms(terms):
    ctx = lax.axis_size("ctx")
    span = terms.shape[0]
    total = terms[span - 1].astype(F32)
    for d in range(1, span):
        moved = lax.ppermute(
            terms[span - 1 - d], "ctx", [(i, (i - d) % ctx) for i in range(ctx)]
        )
        total = total + moved.astype(F32)
    return total.astype(BF16)


def hop(value, dz, of_core):
    pairs = [
        (8 * z + c, 8 * (z ^ dz) + (c ^ of_core[c % 2])) for z in range(4) for c in range(8)
    ]
    return lax.ppermute(value, ("dp", "ctx"), pairs)


FIRST, SECOND, DIAGONAL, STAY, SIBLING = (2, 4), (4, 2), (6, 6), (0, 0), (1, 1)


def gather_pairs(cols):
    both = jnp.stack([cols, hop(cols, 1, STAY)])
    from_first = hop(both, 0, FIRST)
    from_second = hop(both, 0, SECOND)
    from_diagonal = hop(from_first, 0, SECOND)
    kept = [both, from_first, from_second, from_diagonal]
    return kept + [hop(k, 0, SIBLING) for k in kept]


def shards_cube(normed_input, queries, keys_values, grad_output, doc_lengths):
    ctx, dp = lax.axis_size("ctx"), lax.axis_size("dp")
    own, z = lax.axis_index("ctx"), lax.axis_index("dp")
    pieces = spread(jnp.stack([z, own]), normed_input[0], ctx, dp)
    grad_query, terms = attend(own, queries, keys_values, grad_output, doc_lengths)
    chips = (STAY, FIRST, SECOND, DIAGONAL)
    kept = [pieces[0]] + [hop(pieces[i], 0, chips[i]) for i in range(1, 4)]
    kept += [hop(pieces[4 + i], 1, chips[i]) for i in range(4)]
    siblings = [
        hop(jnp.stack([k[1] for k in kept[4 * far : 4 * far + 4]]), 0, SIBLING)
        for far in range(2)
    ]
    turned = turn(kept, siblings)
    side = (z // 2)[None]
    grad_kv = sum_terms(terms)
    totals = []
    for cols in (grad_query, grad_kv):
        gathered = gather_pairs(cols)
        sent = hop(fold(1 - side, turned, gathered, BF16), 2, STAY)
        totals.append(fold(side, turned, gathered, F32) + sent.astype(F32))
    return grad_query[None], grad_kv[None], jnp.concatenate(totals, axis=1)


def shards(normed_input, queries, keys_values, grad_output, doc_lengths):
    ctx = lax.axis_size("ctx")
    own = lax.axis_index("ctx")
    shard_rows, model_width = normed_input.shape[1:]
    grad_query, terms = attend(own, queries, keys_values, grad_output, doc_lengths)
    grad_kv = sum_terms(terms)
    grad_cols = jnp.concatenate([grad_query, grad_kv], axis=1)
    part = model_width // ctx
    pieces = normed_input[0].reshape(shard_rows, ctx, part)
    my_features = lax.all_to_all(pieces, "ctx", split_axis=1, concat_axis=0, tiled=True)
    my_features = my_features.reshape(ctx * shard_rows, part)
    partial = fold_rows(my_features, lax.all_gather(grad_cols, "ctx", axis=0, tiled=True))
    grad_weights = lax.psum_scatter(
        partial.astype(BF16), "dp", scatter_dimension=0, tiled=True
    ).astype(F32)
    return grad_query[None], grad_kv[None], grad_weights


def solution(mesh):
    cube = mesh.shape["dp"] == 4 and mesh.shape["ctx"] == 8
    spec = P("dp", "ctx", None)
    return jax.shard_map(
        shards_cube if cube else shards,
        mesh=mesh,
        in_specs=(spec, spec, spec, spec, P("dp", None)),
        out_specs=(spec, spec, P(("ctx", "dp"), None)),
        check_vma=False,
    )
```

```python
import functools

import jax
import jax.numpy as jnp
from jax import lax
from jax.experimental import pallas as pl
from jax.experimental.pallas import tpu as pltpu
from jax.sharding import PartitionSpec as P

F32 = jnp.float32
BF16 = jnp.bfloat16
VMEM_LIMIT = 16 * 1024 * 1024


def dot(a, b, ca, cb):
    return lax.dot_general(a, b, (((ca,), (cb,)), ((), ())), preferred_element_type=F32)


def attention_kernel(own_ref, lens_ref, q_ref, do_ref, *refs, span, head, group, docs):
    kv_refs, (gq_ref, terms_ref) = refs[:span], refs[span:]
    rows = q_ref.shape[0]
    scale = head ** (-0.5)
    own = own_ref[0]
    first = jnp.int32(0)
    start = jnp.int32(0)
    for d in range(docs):
        first = jnp.where(start <= own, jnp.maximum(first, start), first)
        start = start + lens_ref[0, d]
    kv = jnp.concatenate([r[...] for r in kv_refs], axis=0)
    keys, values = kv[:, :head], kv[:, head:]
    keys_t = keys.T
    width = 2 * rows
    key_at = lax.broadcasted_iota(jnp.int32, (span * rows, width), 0)
    query_at = lax.broadcasted_iota(jnp.int32, (span * rows, width), 1) % rows
    low = (first - own + span - 1) * rows
    allowed = (key_at >= low) & (key_at <= query_at + (span - 1) * rows)
    dk = jnp.zeros((span * rows, head), F32)
    dv = jnp.zeros((span * rows, head), F32)
    for pair in range(group // 2):
        at = [2 * pair * head, (2 * pair + 1) * head]
        q2 = jnp.concatenate([q_ref[:, a : a + head] for a in at], axis=0)
        do2 = jnp.concatenate([do_ref[:, a : a + head] for a in at], axis=0)
        scores = jnp.where(allowed, dot(keys, q2, 1, 1) * scale, -1e30)
        exps = jnp.exp(scores - jnp.max(scores, axis=0, keepdims=True))
        probs = exps * (1.0 / jnp.sum(exps, axis=0, keepdims=True))
        probs_half = probs.astype(BF16)
        dprobs = dot(values, do2, 1, 1)
        row_dots = jnp.sum(probs_half.astype(F32) * dprobs, axis=0, keepdims=True)
        dscores_half = (probs * (dprobs - row_dots)).astype(BF16)
        dk = dk + dot(dscores_half, q2, 1, 0)
        dv = dv + dot(probs_half, do2, 1, 0)
        gq_t = dot(keys_t, dscores_half, 1, 0) * scale
        for i, a in enumerate(at):
            gq_ref[:, a : a + head] = gq_t[:, i * rows : (i + 1) * rows].T.astype(BF16)
    terms_ref[:, :, :head] = (dk * scale).astype(BF16).reshape(span, rows, head)
    terms_ref[:, :, head:] = dv.astype(BF16).reshape(span, rows, head)


def attention(own, lens, q, do, slots, head):
    span, rows = len(slots), q.shape[0]
    group = q.shape[1] // head
    smem = pl.BlockSpec(memory_space=pltpu.SMEM)
    vmem = pl.BlockSpec(memory_space=pltpu.VMEM)
    return pl.pallas_call(
        functools.partial(
            attention_kernel, span=span, head=head, group=group, docs=lens.shape[1]
        ),
        out_shape=(
            jax.ShapeDtypeStruct(q.shape, BF16),
            jax.ShapeDtypeStruct((span, rows, 2 * head), BF16),
        ),
        in_specs=[smem, smem] + [vmem] * (2 + span),
        out_specs=(vmem, vmem),
        compiler_params=pltpu.CompilerParams(vmem_limit_bytes=VMEM_LIMIT),
        cost_estimate=pl.CostEstimate(
            flops=12 * group * rows * rows * span * head,
            bytes_accessed=6 * q.size + 4 * span * rows * 2 * head,
            transcendentals=group * rows * rows * span,
        ),
        name="attention",
    )(own, lens, q, do, *slots)


def spread_kernel(place_ref, x_ref, *outs, dp, part):
    z, c = place_ref[0], place_ref[1]
    first = 2 + 2 * (c % 2)
    chips = (0, first, 6 - first, 6)
    for far in range(2):
        for at, flip in enumerate(chips):
            for other in range(2):
                dest = c ^ flip ^ other
                for high in range(2):
                    plane = (2 * high + z % 2) ^ far
                    src = pl.multiple_of((dest * dp + plane) * part, part)
                    outs[4 * far + at][other, :, high * part : (high + 1) * part] = x_ref[
                        :, pl.ds(src, part)
                    ]


def spread(place, x, ctx, dp):
    rows, width = x.shape
    part = width // (ctx * dp)
    piece = jax.ShapeDtypeStruct((2, rows, 2 * part), BF16)
    vmem = pl.BlockSpec(memory_space=pltpu.VMEM)
    return pl.pallas_call(
        functools.partial(spread_kernel, dp=dp, part=part),
        out_shape=(piece,) * 8,
        in_specs=[pl.BlockSpec(memory_space=pltpu.SMEM), vmem],
        out_specs=(vmem,) * 8,
        compiler_params=pltpu.CompilerParams(vmem_limit_bytes=VMEM_LIMIT),
        cost_estimate=pl.CostEstimate(flops=0, bytes_accessed=4 * x.size, transcendentals=0),
        name="spread",
    )(place, x)


def turn_kernel(*refs):
    kept, siblings, out = refs[:8], refs[8:10], refs[10]
    rows = kept[0].shape[1]
    for at in range(4):
        for far in range(2):
            j = 2 * at + far
            out[:, j * rows : (j + 1) * rows] = kept[4 * far + at][0].T
            out[:, (8 + j) * rows : (9 + j) * rows] = siblings[far][at].T


def turn(kept, siblings):
    _, rows, width = kept[0].shape
    vmem = pl.BlockSpec(memory_space=pltpu.VMEM)
    return pl.pallas_call(
        turn_kernel,
        out_shape=jax.ShapeDtypeStruct((width, 16 * rows), BF16),
        in_specs=[vmem] * 10,
        out_specs=vmem,
        compiler_params=pltpu.CompilerParams(vmem_limit_bytes=VMEM_LIMIT),
        cost_estimate=pl.CostEstimate(
            flops=0, bytes_accessed=64 * rows * width, transcendentals=0
        ),
        name="turn",
    )(*kept, *siblings)


def fold_kernel(side_ref, x_ref, *refs):
    cols, out = refs[:-1], refs[-1]
    depth = cols[0].shape[0] * cols[0].shape[1]
    half = out.shape[0]
    at = pl.multiple_of(side_ref[0] * half, half)
    total = None
    for j, col in enumerate(cols):
        block = col[...].reshape(depth, col.shape[2])
        term = dot(x_ref[pl.ds(at, half), j * depth : (j + 1) * depth], block, 1, 0)
        total = term if total is None else total + term
    out[...] = total.astype(out.dtype)


def fold(side, turned, cols, dtype):
    width, depth = turned.shape
    half = width // 2
    n = cols[0].shape[2]
    vmem = pl.BlockSpec(memory_space=pltpu.VMEM)
    return pl.pallas_call(
        fold_kernel,
        in_specs=[pl.BlockSpec(memory_space=pltpu.SMEM)] + [vmem] * (1 + len(cols)),
        out_specs=vmem,
        out_shape=jax.ShapeDtypeStruct((half, n), dtype),
        compiler_params=pltpu.CompilerParams(vmem_limit_bytes=VMEM_LIMIT),
        cost_estimate=pl.CostEstimate(
            flops=2 * half * depth * n,
            bytes_accessed=2 * half * depth + 2 * depth * n + 4 * half * n,
            transcendentals=0,
        ),
        name="fold",
    )(side, turned, *cols)


def fold_rows(features, piece_rows):
    return lax.dot_general(
        features, piece_rows, (((0,), (0,)), ((), ())), preferred_element_type=F32
    )


def attend(own_index, queries, keys_values, grad_output, doc_lengths):
    ctx = lax.axis_size("ctx")
    span = ctx // 2 + 1
    own_kv = keys_values[0]
    slots = [own_kv]
    for d in range(1, span):
        moved = lax.ppermute(own_kv, "ctx", [(i, (i + d) % ctx) for i in range(ctx)])
        slots.insert(0, moved)
    head = keys_values.shape[2] // 2
    return attention(
        own_index[None], doc_lengths, queries[0], grad_output[0], slots, head
    )


def sum_terms(terms):
    ctx = lax.axis_size("ctx")
    span = terms.shape[0]
    total = terms[span - 1].astype(F32)
    for d in range(1, span):
        moved = lax.ppermute(
            terms[span - 1 - d], "ctx", [(i, (i - d) % ctx) for i in range(ctx)]
        )
        total = total + moved.astype(F32)
    return total.astype(BF16)


def hop(value, dz, of_core):
    pairs = [
        (8 * z + c, 8 * (z ^ dz) + (c ^ of_core[c % 2])) for z in range(4) for c in range(8)
    ]
    return lax.ppermute(value, ("dp", "ctx"), pairs)


FIRST, SECOND, DIAGONAL, STAY, SIBLING = (2, 4), (4, 2), (6, 6), (0, 0), (1, 1)


def gather_pairs(cols):
    both = jnp.stack([cols, hop(cols, 1, STAY)])
    from_first = hop(both, 0, FIRST)
    from_second = hop(both, 0, SECOND)
    from_diagonal = hop(from_first, 0, SECOND)
    kept = [both, from_first, from_second, from_diagonal]
    return kept + [hop(k, 0, SIBLING) for k in kept]


def shards_cube(normed_input, queries, keys_values, grad_output, doc_lengths):
    ctx, dp = lax.axis_size("ctx"), lax.axis_size("dp")
    own, z = lax.axis_index("ctx"), lax.axis_index("dp")
    pieces = spread(jnp.stack([z, own]), normed_input[0], ctx, dp)
    grad_query, terms = attend(own, queries, keys_values, grad_output, doc_lengths)
    chips = (STAY, FIRST, SECOND, DIAGONAL)
    kept = [pieces[0]] + [hop(pieces[i], 0, chips[i]) for i in range(1, 4)]
    kept += [hop(pieces[4 + i], 1, chips[i]) for i in range(4)]
    siblings = [
        hop(jnp.stack([k[1] for k in kept[4 * far : 4 * far + 4]]), 0, SIBLING)
        for far in range(2)
    ]
    turned = turn(kept, siblings)
    side = (z // 2)[None]
    grad_kv = sum_terms(terms)
    totals = []
    half = grad_query.shape[1] // 2
    for cols in (grad_query[:, :half], grad_query[:, half:], grad_kv):
        gathered = gather_pairs(cols)
        sent = hop(fold(1 - side, turned, gathered, BF16), 2, STAY)
        totals.append(fold(side, turned, gathered, F32) + sent.astype(F32))
    return grad_query[None], grad_kv[None], jnp.concatenate(totals, axis=1)


def shards(normed_input, queries, keys_values, grad_output, doc_lengths):
    ctx = lax.axis_size("ctx")
    own = lax.axis_index("ctx")
    shard_rows, model_width = normed_input.shape[1:]
    grad_query, terms = attend(own, queries, keys_values, grad_output, doc_lengths)
    grad_kv = sum_terms(terms)
    grad_cols = jnp.concatenate([grad_query, grad_kv], axis=1)
    part = model_width // ctx
    pieces = normed_input[0].reshape(shard_rows, ctx, part)
    my_features = lax.all_to_all(pieces, "ctx", split_axis=1, concat_axis=0, tiled=True)
    my_features = my_features.reshape(ctx * shard_rows, part)
    partial = fold_rows(my_features, lax.all_gather(grad_cols, "ctx", axis=0, tiled=True))
    grad_weights = lax.psum_scatter(
        partial.astype(BF16), "dp", scatter_dimension=0, tiled=True
    ).astype(F32)
    return grad_query[None], grad_kv[None], grad_weights


def solution(mesh):
    cube = mesh.shape["dp"] == 4 and mesh.shape["ctx"] == 8
    spec = P("dp", "ctx", None)
    return jax.shard_map(
        shards_cube if cube else shards,
        mesh=mesh,
        in_specs=(spec, spec, spec, spec, P("dp", None)),
        out_specs=(spec, spec, P(("ctx", "dp"), None)),
        check_vma=False,
    )
```

```python
import functools

import jax
import jax.numpy as jnp
from jax import lax
from jax.experimental import pallas as pl
from jax.experimental.pallas import tpu as pltpu
from jax.sharding import PartitionSpec as P

F32 = jnp.float32
BF16 = jnp.bfloat16
VMEM_LIMIT = 16 * 1024 * 1024
LEAD = 4


def dot(a, b, ca, cb):
    return lax.dot_general(a, b, (((ca,), (cb,)), ((), ())), preferred_element_type=F32)


def attention_kernel(own_ref, lens_ref, q_ref, do_ref, *refs, span, head, group, docs, cube):
    kv_refs, (gq_ref, lead_ref), term_refs = refs[:span], refs[span : span + 2], refs[span + 2 :]
    rows = q_ref.shape[0]
    scale = head ** (-0.5)
    own = own_ref[0]
    first = jnp.int32(0)
    start = jnp.int32(0)
    for d in range(docs):
        first = jnp.where(start <= own, jnp.maximum(first, start), first)
        start = start + lens_ref[0, d]
    kv = jnp.concatenate([r[...] for r in kv_refs], axis=0)
    keys, values = kv[:, :head], kv[:, head:]
    keys_t = keys.T
    width = 2 * rows
    key_at = lax.broadcasted_iota(jnp.int32, (span * rows, width), 0)
    query_at = lax.broadcasted_iota(jnp.int32, (span * rows, width), 1) % rows
    low = (first - own + span - 1) * rows
    allowed = (key_at >= low) & (key_at <= query_at + (span - 1) * rows)
    dk = jnp.zeros((span * rows, head), F32)
    dv = jnp.zeros((span * rows, head), F32)
    for pair in range(group // 2):
        at = [2 * pair * head, (2 * pair + 1) * head]
        q2 = jnp.concatenate([q_ref[:, a : a + head] for a in at], axis=0)
        do2 = jnp.concatenate([do_ref[:, a : a + head] for a in at], axis=0)
        scores = jnp.where(allowed, dot(keys, q2, 1, 1) * scale, -1e30)
        exps = jnp.exp(scores - jnp.max(scores, axis=0, keepdims=True))
        probs = exps * (1.0 / jnp.sum(exps, axis=0, keepdims=True))
        probs_half = probs.astype(BF16)
        dprobs = dot(values, do2, 1, 1)
        row_dots = jnp.sum(probs_half.astype(F32) * dprobs, axis=0, keepdims=True)
        dscores_half = (probs * (dprobs - row_dots)).astype(BF16)
        dk = dk + dot(dscores_half, q2, 1, 0)
        dv = dv + dot(probs_half, do2, 1, 0)
        gq_t = dot(keys_t, dscores_half, 1, 0) * scale
        for i, a in enumerate(at):
            gq = gq_t[:, i * rows : (i + 1) * rows].T.astype(BF16)
            gq_ref[:, a : a + head] = gq
            if a < lead_ref.shape[1]:
                lead_ref[:, a : a + head] = gq
    terms = jnp.concatenate([dk * scale, dv], axis=1).astype(BF16).reshape(span, rows, 2 * head)
    if not cube:
        term_refs[0][...] = terms
        term_refs[1][...] = terms[span - 1]
        return
    for ref in term_refs:
        ref[...] = jnp.zeros_like(ref)
    for t in range(span):
        p = cube_place(own, own - (span - 1) + t)
        shown = own >= span - 1 - t

        for chip, ref in enumerate(term_refs):

            @pl.when(shown & (p // 2 == chip))
            def _(t=t, p=p, ref=ref):
                ref[p % 2] = terms[t].astype(ref.dtype)


def cube_place(own, shard):
    gap = jnp.bitwise_xor(own, shard % 8)
    core, across, along = gap % 2, gap // 2 % 2, gap // 4
    first = jnp.where(own % 2 == 0, across, along)
    return core + 2 * first + 4 * (across + along - first)


def shift(value, by):
    ctx = lax.axis_size("ctx")
    return lax.ppermute(value, "ctx", [(i, (i + by) % ctx) for i in range(ctx)])


def attention(own, lens, q, do, own_kv, cube):
    ctx = lax.axis_size("ctx")
    span = ctx // 2 + 1
    slots = [shift(own_kv, d) for d in range(span - 1, 0, -1)] + [own_kv]
    head = own_kv.shape[1] // 2
    rows = q.shape[0]
    group = q.shape[1] // head
    smem = pl.BlockSpec(memory_space=pltpu.SMEM)
    vmem = pl.BlockSpec(memory_space=pltpu.VMEM)
    if cube:
        terms = [jax.ShapeDtypeStruct((2, rows, 2 * head), t) for t in (F32, BF16, BF16, BF16)]
    else:
        terms = [jax.ShapeDtypeStruct(n + (rows, 2 * head), BF16) for n in ((span,), ())]
    return pl.pallas_call(
        functools.partial(
            attention_kernel, span=span, head=head, group=group, docs=lens.shape[1], cube=cube
        ),
        out_shape=(
            jax.ShapeDtypeStruct(q.shape, BF16),
            jax.ShapeDtypeStruct((rows, LEAD * head), BF16),
            *terms,
        ),
        in_specs=[smem, smem] + [vmem] * (2 + len(slots)),
        out_specs=(vmem,) * (2 + len(terms)),
        compiler_params=pltpu.CompilerParams(vmem_limit_bytes=VMEM_LIMIT),
        cost_estimate=pl.CostEstimate(
            flops=12 * group * rows * rows * span * head,
            bytes_accessed=6 * q.size + 4 * span * rows * 2 * head,
            transcendentals=group * rows * rows * span,
        ),
        name="attention",
    )(own, lens, q, do, *slots)


def spread_kernel(place_ref, x_ref, *outs, dp, part):
    z, c = place_ref[0], place_ref[1]
    first = 2 + 2 * (c % 2)
    for far in range(2):
        for at, flip in enumerate((0, first, 6 - first, 6)):
            out = outs[at] if not far else outs[5] if at == 3 else outs[4].at[at]
            for other in range(2):
                for high in range(2):
                    plane = (2 * high + z % 2) ^ far
                    src = pl.multiple_of(((c ^ flip ^ other) * dp + plane) * part, part)
                    out[other, :, high * part : (high + 1) * part] = x_ref[:, pl.ds(src, part)]


def spread(place, x, ctx, dp):
    rows, width = x.shape
    part = width // (ctx * dp)
    piece = (2, rows, 2 * part)
    vmem = pl.BlockSpec(memory_space=pltpu.VMEM)
    return pl.pallas_call(
        functools.partial(spread_kernel, dp=dp, part=part),
        out_shape=[jax.ShapeDtypeStruct(p, BF16) for p in [piece] * 4 + [(3,) + piece, piece]],
        in_specs=[pl.BlockSpec(memory_space=pltpu.SMEM), vmem],
        out_specs=[vmem] * 6,
        compiler_params=pltpu.CompilerParams(vmem_limit_bytes=VMEM_LIMIT),
        cost_estimate=pl.CostEstimate(flops=0, bytes_accessed=4 * x.size, transcendentals=0),
        name="spread",
    )(place, x)


def local_call(kernel, name, out_shape, args, gates=(), smem=0, flops=0):
    vmem = pl.BlockSpec(memory_space=pltpu.VMEM)
    specs = [pl.BlockSpec(memory_space=pltpu.SMEM)] * smem + [vmem] * (len(args) - smem)
    specs += [pl.BlockSpec(memory_space=pl.ANY)] * len(gates)
    return pl.pallas_call(
        kernel,
        out_shape=out_shape,
        in_specs=specs,
        out_specs=jax.tree.map(lambda _: vmem, out_shape),
        compiler_params=pltpu.CompilerParams(vmem_limit_bytes=VMEM_LIMIT),
        cost_estimate=pl.CostEstimate(
            flops=flops,
            bytes_accessed=sum(2 * a.size for a in args) + sum(2 * o.size for o in out_shape),
            transcendentals=0,
        ),
        name=name,
    )(*args, *gates)


def turn_kernel(*refs):
    pieces, outs = refs[:4], refs[-2:]
    rows = pieces[1].shape[1]
    for at, piece in enumerate(pieces):
        piece = piece.at[0] if len(piece.shape) == 4 else piece
        for core in range(2):
            outs[core][:, at * rows : (at + 1) * rows] = piece[core].T


def turn(pieces):
    _, rows, width = pieces[1].shape
    turned = jax.ShapeDtypeStruct((width, 4 * rows), BF16)
    return local_call(turn_kernel, "turn", (turned, turned), pieces)


def pack_kernel(own_ref, moved_ref, *refs):
    n = own_ref.shape[0]
    refs[-1][:n] = own_ref[...]
    refs[-1][n:] = moved_ref[...]


def pack(own, moved, gates=()):
    out = jax.ShapeDtypeStruct((2 * own.shape[0],) + own.shape[1:], BF16)
    return local_call(pack_kernel, "pack", (out,), [own, moved], gates)[0]


def hold_kernel(own_ref, *refs):
    refs[-1][...] = own_ref[...]


def hold(own, gates):
    out = jax.ShapeDtypeStruct(own.shape, own.dtype)
    return local_call(hold_kernel, "hold", (out,), [own], gates)[0]


def merge_kernel(held_ref, *refs):
    moved, (hold_ref, send_ref) = refs[:3], refs[-2:]
    total = held_ref[...]
    for ref in moved:
        total = total + ref[...].astype(F32)
    hold_ref[...] = total[0]
    send_ref[...] = total[1].astype(BF16)


def merge(held, moved, gates=()):
    outs = tuple(jax.ShapeDtypeStruct(held.shape[1:], t) for t in (F32, BF16))
    return local_call(merge_kernel, "merge", outs, [held, *moved], gates)


def settle_kernel(gq_ref, held_ref, *refs):
    moved, (cols_ref, gkv_ref) = refs[:-2], refs[-2:]
    width = cols_ref.shape[1] - gkv_ref.shape[1]
    total = held_ref[...].astype(F32)
    for ref in moved:
        total = total + ref[...].astype(F32)
    gkv = total.astype(BF16)
    gkv_ref[...] = gkv
    cols_ref[:, :width] = gq_ref[:, gq_ref.shape[1] - width :]
    cols_ref[:, width:] = gkv


def settle(gq, lead, held, moved):
    rows, kv_width = held.shape
    outs = (
        jax.ShapeDtypeStruct((rows, gq.shape[1] - lead.shape[1] + kv_width), BF16),
        jax.ShapeDtypeStruct((rows, kv_width), BF16),
    )
    return local_call(settle_kernel, "settle", outs, [gq, held, *moved])


def fold_kernel(side_ref, *refs):
    turned, cols, out = refs[:4], refs[4:10], refs[-1]
    rows = cols[0].shape[1]
    pairs = [(col, at) for col in cols for at in range(0, col.shape[0], 2)]
    half, n = out.shape
    at = pl.multiple_of(side_ref[0] * half, half)
    total = None
    for core in range(2):
        for chip in range(4):
            span = slice(chip * rows, (chip + 1) * rows)
            left = jnp.concatenate(
                [t[pl.ds(at, half), span] for t in turned[2 * core : 2 * core + 2]], axis=1
            )
            col, pair = pairs[4 * core + chip]
            term = dot(left, col[pair : pair + 2].reshape(2 * rows, n), 1, 0)
            total = term if total is None else total + term
    out[...] = total.astype(out.dtype)


def fold(side, turned, cols, dtype, gates=()):
    half = turned[0].shape[0] // 2
    depth = 4 * turned[0].shape[1]
    n = cols[0].shape[2]
    out = jax.ShapeDtypeStruct((half, n), dtype)
    args = [side, *turned, *cols]
    flops = 2 * half * depth * n
    return local_call(fold_kernel, "fold", (out,), args, gates, smem=1, flops=flops)[0]


def fold_rows(features, piece_rows):
    return lax.dot_general(
        features, piece_rows, (((0,), (0,)), ((), ())), preferred_element_type=F32
    )


def hop(value, dz, of_core):
    pairs = [
        (8 * z + c, 8 * (z ^ dz) + (c ^ of_core[c % 2])) for z in range(4) for c in range(8)
    ]
    return lax.ppermute(value, ("dp", "ctx"), pairs)


FIRST, SECOND, DIAGONAL, STAY, SIBLING = (2, 4), (4, 2), (6, 6), (0, 0), (1, 1)


def gather_pairs(cols, gates, late_gates=()):
    both = pack(cols[None], hop(cols, 1, STAY)[None], gates)
    from_first = hop(both, 0, FIRST)
    from_second = hop(both, 0, SECOND)
    from_diagonal = hop(from_first, 0, SECOND)
    near = hop(pack(both, from_first), 0, SIBLING)
    far = hop(pack(from_second, from_diagonal, late_gates), 0, SIBLING)
    return [both, from_first, from_second, from_diagonal, near, far]


def shards_cube(normed_input, queries, keys_values, grad_output, doc_lengths):
    ctx, dp = lax.axis_size("ctx"), lax.axis_size("dp")
    own, z = lax.axis_index("ctx"), lax.axis_index("dp")
    side = (z // 2)[None]
    *pieces, across, corner = spread(jnp.stack([z, own]), normed_input[0], ctx, dp)
    grad_query, lead, held, *send = attention(
        own[None], doc_lengths, queries[0], grad_output[0], keys_values[0], cube=True
    )
    chips = (FIRST, SECOND, DIAGONAL)
    near, near_sib = turn(pieces[:1] + [hop(p, 0, c) for p, c in zip(pieces[1:], chips)])
    across = hop(across, 1, STAY)
    corner = hop(hold(corner, [lead]), 1, DIAGONAL)
    far, far_sib = turn([across, hop(across[1], 0, FIRST), hop(across[2], 0, SECOND), corner])
    turned = [near, far, hop(near_sib, 0, SIBLING), hop(far_sib, 0, SIBLING)]
    first_cols = gather_pairs(lead, [near])
    held, send = merge(held, [hop(t, 0, c) for t, c in zip(send, chips)])
    rest, grad_kv = settle(grad_query, lead, held, [hop(send, 0, SIBLING)])
    first_fold = fold(1 - side, turned, first_cols, BF16)
    rest_cols = gather_pairs(rest, [far], [first_fold])
    first_sent = hop(first_fold, 2, STAY)
    rest_sent = hop(fold(1 - side, turned, rest_cols, BF16), 2, STAY)
    totals = [
        fold(side, turned, cols, F32) + sent.astype(F32)
        for cols, sent in ((first_cols, first_sent), (rest_cols, rest_sent))
    ]
    return grad_query[None], grad_kv[None], jnp.concatenate(totals, axis=1)


def shards(normed_input, queries, keys_values, grad_output, doc_lengths):
    ctx = lax.axis_size("ctx")
    own = lax.axis_index("ctx")
    shard_rows, model_width = normed_input.shape[1:]
    grad_query, lead, terms, held = attention(
        own[None], doc_lengths, queries[0], grad_output[0], keys_values[0], cube=False
    )
    span = terms.shape[0]
    moved = [shift(terms[span - 1 - d], -d) for d in range(1, span)]
    rest, grad_kv = settle(grad_query, lead, held, moved)
    grad_cols = jnp.concatenate([lead, rest], axis=1)
    part = model_width // ctx
    pieces = normed_input[0].reshape(shard_rows, ctx, part)
    my_features = lax.all_to_all(pieces, "ctx", split_axis=1, concat_axis=0, tiled=True)
    my_features = my_features.reshape(ctx * shard_rows, part)
    partial = fold_rows(my_features, lax.all_gather(grad_cols, "ctx", axis=0, tiled=True))
    grad_weights = lax.psum_scatter(
        partial.astype(BF16), "dp", scatter_dimension=0, tiled=True
    ).astype(F32)
    return grad_query[None], grad_kv[None], grad_weights


def solution(mesh):
    cube = mesh.shape["dp"] == 4 and mesh.shape["ctx"] == 8
    spec = P("dp", "ctx", None)
    return jax.shard_map(
        shards_cube if cube else shards,
        mesh=mesh,
        in_specs=(spec, spec, spec, spec, P("dp", None)),
        out_specs=(spec, spec, P(("ctx", "dp"), None)),
        check_vma=False,
    )
```

```python
import functools

import jax
import jax.numpy as jnp
from jax import lax
from jax.experimental import pallas as pl
from jax.experimental.pallas import tpu as pltpu
from jax.sharding import PartitionSpec as P

F32 = jnp.float32
BF16 = jnp.bfloat16
VMEM_LIMIT = 16 * 1024 * 1024
LEAD = 4


def dot(a, b, ca, cb):
    return lax.dot_general(a, b, (((ca,), (cb,)), ((), ())), preferred_element_type=F32)


def attention_kernel(own_ref, lens_ref, q_ref, do_ref, *refs, span, head, group, docs, cube):
    kv_refs, (gq_ref, lead_ref), term_refs = refs[:span], refs[span : span + 2], refs[span + 2 :]
    rows = q_ref.shape[0]
    scale = head ** (-0.5)
    own = own_ref[0]
    first = jnp.int32(0)
    start = jnp.int32(0)
    for d in range(docs):
        first = jnp.where(start <= own, jnp.maximum(first, start), first)
        start = start + lens_ref[0, d]
    kv = jnp.concatenate([r[...] for r in kv_refs], axis=0)
    keys, values = kv[:, :head], kv[:, head:]
    keys_t = keys.T
    width = 2 * rows
    key_at = lax.broadcasted_iota(jnp.int32, (span * rows, width), 0)
    query_at = lax.broadcasted_iota(jnp.int32, (span * rows, width), 1) % rows
    low = (first - own + span - 1) * rows
    allowed = (key_at >= low) & (key_at <= query_at + (span - 1) * rows)
    dk = jnp.zeros((span * rows, head), F32)
    dv = jnp.zeros((span * rows, head), F32)
    for pair in range(group // 2):
        at = [2 * pair * head, (2 * pair + 1) * head]
        q2 = jnp.concatenate([q_ref[:, a : a + head] for a in at], axis=0)
        do2 = jnp.concatenate([do_ref[:, a : a + head] for a in at], axis=0)
        scores = jnp.where(allowed, dot(keys, q2, 1, 1) * scale, -1e30)
        exps = jnp.exp(scores - jnp.max(scores, axis=0, keepdims=True))
        probs = exps * (1.0 / jnp.sum(exps, axis=0, keepdims=True))
        probs_half = probs.astype(BF16)
        dprobs = dot(values, do2, 1, 1)
        row_dots = jnp.sum(probs_half.astype(F32) * dprobs, axis=0, keepdims=True)
        dscores_half = (probs * (dprobs - row_dots)).astype(BF16)
        dk = dk + dot(dscores_half, q2, 1, 0)
        dv = dv + dot(probs_half, do2, 1, 0)
        gq_t = dot(keys_t, dscores_half, 1, 0) * scale
        for i, a in enumerate(at):
            gq = gq_t[:, i * rows : (i + 1) * rows].T.astype(BF16)
            gq_ref[:, a : a + head] = gq
            if a < lead_ref.shape[1]:
                lead_ref[:, a : a + head] = gq
    terms = jnp.concatenate([dk * scale, dv], axis=1).astype(BF16).reshape(span, rows, 2 * head)
    if not cube:
        term_refs[0][...] = terms
        term_refs[1][...] = terms[span - 1]
        return
    for ref in term_refs:
        ref[...] = jnp.zeros_like(ref)
    for t in range(span):
        p = cube_place(own, own - (span - 1) + t)
        shown = own >= span - 1 - t

        for chip, ref in enumerate(term_refs):

            @pl.when(shown & (p // 2 == chip))
            def _(t=t, p=p, ref=ref):
                ref[p % 2] = terms[t].astype(ref.dtype)


def cube_place(own, shard):
    gap = jnp.bitwise_xor(own, shard % 8)
    core, across, along = gap % 2, gap // 2 % 2, gap // 4
    first = jnp.where(own % 2 == 0, across, along)
    return core + 2 * first + 4 * (across + along - first)


def shift(value, by):
    ctx = lax.axis_size("ctx")
    return lax.ppermute(value, "ctx", [(i, (i + by) % ctx) for i in range(ctx)])


def attention(own, lens, q, do, own_kv, cube):
    ctx = lax.axis_size("ctx")
    span = ctx // 2 + 1
    slots = [shift(own_kv, d) for d in range(span - 1, 0, -1)] + [own_kv]
    head = own_kv.shape[1] // 2
    rows = q.shape[0]
    group = q.shape[1] // head
    smem = pl.BlockSpec(memory_space=pltpu.SMEM)
    vmem = pl.BlockSpec(memory_space=pltpu.VMEM)
    if cube:
        terms = [jax.ShapeDtypeStruct((2, rows, 2 * head), t) for t in (F32, BF16, BF16, BF16)]
    else:
        terms = [jax.ShapeDtypeStruct(n + (rows, 2 * head), BF16) for n in ((span,), ())]
    return pl.pallas_call(
        functools.partial(
            attention_kernel, span=span, head=head, group=group, docs=lens.shape[1], cube=cube
        ),
        out_shape=(
            jax.ShapeDtypeStruct(q.shape, BF16),
            jax.ShapeDtypeStruct((rows, LEAD * head), BF16),
            *terms,
        ),
        in_specs=[smem, smem] + [vmem] * (2 + len(slots)),
        out_specs=(vmem,) * (2 + len(terms)),
        compiler_params=pltpu.CompilerParams(vmem_limit_bytes=VMEM_LIMIT),
        cost_estimate=pl.CostEstimate(
            flops=12 * group * rows * rows * span * head,
            bytes_accessed=6 * q.size + 4 * span * rows * 2 * head,
            transcendentals=group * rows * rows * span,
        ),
        name="attention",
    )(own, lens, q, do, *slots)


def spread_kernel(place_ref, x_ref, *outs, dp, part):
    z, c = place_ref[0], place_ref[1]
    first = 2 + 2 * (c % 2)
    for home in range(2):
        for far in range(2):
            for at, flip in enumerate((0, first, 6 - first, 6)):
                if home:
                    out = outs[9].at[at] if far else outs[5 + at]
                else:
                    out = outs[4].at[at] if far else outs[at]
                plane = z ^ far ^ (2 - 2 * home)
                for other in range(2):
                    src = pl.multiple_of(((c ^ flip ^ other) * dp + plane) * part, part)
                    out[other] = x_ref[:, pl.ds(src, part)]


def spread(place, x, ctx, dp):
    rows, width = x.shape
    part = width // (ctx * dp)
    piece = (2, rows, part)
    vmem = pl.BlockSpec(memory_space=pltpu.VMEM)
    shapes = ([piece] * 4 + [(4,) + piece]) * 2
    return pl.pallas_call(
        functools.partial(spread_kernel, dp=dp, part=part),
        out_shape=[jax.ShapeDtypeStruct(p, BF16) for p in shapes],
        in_specs=[pl.BlockSpec(memory_space=pltpu.SMEM), vmem],
        out_specs=[vmem] * len(shapes),
        compiler_params=pltpu.CompilerParams(vmem_limit_bytes=VMEM_LIMIT),
        cost_estimate=pl.CostEstimate(flops=0, bytes_accessed=4 * x.size, transcendentals=0),
        name="spread",
    )(place, x)


def local_call(kernel, name, out_shape, args, gates=(), smem=0, flops=0):
    vmem = pl.BlockSpec(memory_space=pltpu.VMEM)
    specs = [pl.BlockSpec(memory_space=pltpu.SMEM)] * smem + [vmem] * (len(args) - smem)
    specs += [pl.BlockSpec(memory_space=pl.ANY)] * len(gates)
    return pl.pallas_call(
        kernel,
        out_shape=out_shape,
        in_specs=specs,
        out_specs=jax.tree.map(lambda _: vmem, out_shape),
        compiler_params=pltpu.CompilerParams(vmem_limit_bytes=VMEM_LIMIT),
        cost_estimate=pl.CostEstimate(
            flops=flops,
            bytes_accessed=0,
            transcendentals=0,
        ),
        name=name,
    )(*args, *gates)


def turn_kernel(*refs):
    pieces, outs = refs[:4], refs[-2:]
    rows = pieces[1].shape[1]
    for at, piece in enumerate(pieces):
        piece = piece.at[0] if len(piece.shape) == 4 else piece
        for core in range(2):
            outs[core][:, at * rows : (at + 1) * rows] = piece[core].T


def turn(pieces, gates=()):
    _, rows, width = pieces[1].shape
    turned = jax.ShapeDtypeStruct((width, 4 * rows), BF16)
    return local_call(turn_kernel, "turn", (turned, turned), pieces, gates)


def pack_kernel(own_ref, moved_ref, *refs):
    n = own_ref.shape[0]
    refs[-1][:n] = own_ref[...]
    refs[-1][n:] = moved_ref[...]


def pack(own, moved, gates=()):
    out = jax.ShapeDtypeStruct((2 * own.shape[0],) + own.shape[1:], BF16)
    return local_call(pack_kernel, "pack", (out,), [own, moved], gates)[0]


def hold_kernel(*refs, count):
    for own, out in zip(refs[:count], refs[-count:]):
        out[...] = own[...]


def hold(own, gates):
    outs = [jax.ShapeDtypeStruct(a.shape, a.dtype) for a in own]
    kernel = functools.partial(hold_kernel, count=len(own))
    return local_call(kernel, "hold", outs, own, gates)


def merge_kernel(held_ref, *refs):
    moved, (hold_ref, send_ref) = refs[:3], refs[-2:]
    total = held_ref[...]
    for ref in moved:
        total = total + ref[...].astype(F32)
    hold_ref[...] = total[0]
    send_ref[...] = total[1].astype(BF16)


def merge(held, moved, gates=()):
    outs = tuple(jax.ShapeDtypeStruct(held.shape[1:], t) for t in (F32, BF16))
    return local_call(merge_kernel, "merge", outs, [held, *moved], gates)


def settle_kernel(gq_ref, held_ref, *refs):
    moved, (cols_ref, gkv_ref) = refs[:-2], refs[-2:]
    width = cols_ref.shape[1] - gkv_ref.shape[1]
    total = held_ref[...].astype(F32)
    for ref in moved:
        total = total + ref[...].astype(F32)
    gkv = total.astype(BF16)
    gkv_ref[...] = gkv
    cols_ref[:, :width] = gq_ref[:, gq_ref.shape[1] - width :]
    cols_ref[:, width:] = gkv


def settle(gq, lead, held, moved):
    rows, kv_width = held.shape
    outs = (
        jax.ShapeDtypeStruct((rows, gq.shape[1] - lead.shape[1] + kv_width), BF16),
        jax.ShapeDtypeStruct((rows, kv_width), BF16),
    )
    return local_call(settle_kernel, "settle", outs, [gq, held, *moved])


def fold_kernel(*refs, outs, joined):
    turned, cols, outs = refs[:4], refs[4:10], refs[-outs:]
    lead = refs[10] if joined else None
    rows = cols[0].shape[1]
    pairs = [(col, at) for col in cols for at in range(0, col.shape[0], 2)]
    total = None
    for core in range(2):
        for chip in range(4):
            span = slice(chip * rows, (chip + 1) * rows)
            left = jnp.concatenate([t[:, span] for t in turned[2 * core : 2 * core + 2]], axis=1)
            col, pair = pairs[4 * core + chip]
            term = dot(left, col[pair : pair + 2].reshape(2 * rows, col.shape[2]), 1, 0)
            total = term if total is None else total + term
    total = total.astype(outs[0].dtype)
    if joined:
        total = jnp.concatenate([lead[...], total], axis=1)
    start = 0
    for out in outs:
        out[...] = total[:, start : start + out.shape[1]]
        start += out.shape[1]


def fold(turned, cols, dtype, cuts=(), joined=()):
    half, depth = turned[0].shape
    n = cols[0].shape[2] + sum(j.shape[1] for j in joined)
    edges = [0, *cuts, n]
    outs = [jax.ShapeDtypeStruct((half, b - a), dtype) for a, b in zip(edges, edges[1:])]
    kernel = functools.partial(fold_kernel, outs=len(outs), joined=bool(joined))
    return local_call(kernel, "fold", outs, [*turned, *cols, *joined])


def fold_rows(features, piece_rows):
    return lax.dot_general(
        features, piece_rows, (((0,), (0,)), ((), ())), preferred_element_type=F32
    )


def hop(value, dz, of_core):
    pairs = [
        (8 * z + c, 8 * (z ^ dz) + (c ^ of_core[c % 2])) for z in range(4) for c in range(8)
    ]
    return lax.ppermute(value, ("dp", "ctx"), pairs)


FIRST, SECOND, DIAGONAL, STAY, SIBLING = (2, 4), (4, 2), (6, 6), (0, 0), (1, 1)


def gather_pairs(cols, gates, late_gates=()):
    both = pack(cols[None], hop(cols, 1, STAY)[None], gates)
    from_first = hop(both, 0, FIRST)
    from_second = hop(both, 0, SECOND)
    from_diagonal = hop(from_first, 0, SECOND)
    near = hop(pack(both, from_first), 0, SIBLING)
    far = hop(pack(from_second, from_diagonal, late_gates), 0, SIBLING)
    return [both, from_first, from_second, from_diagonal, near, far]


def shards_cube(normed_input, queries, keys_values, grad_output, doc_lengths):
    ctx, dp = lax.axis_size("ctx"), lax.axis_size("dp")
    own, z = lax.axis_index("ctx"), lax.axis_index("dp")
    pieces = spread(jnp.stack([z, own]), normed_input[0], ctx, dp)
    grad_query, lead, held, *send = attention(
        own[None], doc_lengths, queries[0], grad_output[0], keys_values[0], cube=True
    )
    chips = (FIRST, SECOND, DIAGONAL)
    near, near_sib = turn([pieces[0]] + [hop(p, 0, c) for p, c in zip(pieces[1:4], chips)])
    across = hop(pieces[4], 1, STAY)
    far, far_sib = turn([across] + [hop(across[i + 1], 0, c) for i, c in enumerate(chips)])
    away = [near, far, hop(near_sib, 0, SIBLING), hop(far_sib, 0, SIBLING)]
    first_cols = gather_pairs(lead, [near])
    beyond = hop(hold([pieces[9]], [first_cols[0]])[0], 1, STAY)
    held, send = merge(held, [hop(t, 0, c) for t, c in zip(send, chips)])
    rest, grad_kv = settle(grad_query, lead, held, [hop(send, 0, SIBLING)])
    first_folds = fold(away, first_cols, BF16, cuts=[256])
    sent = [hop(first_folds[0], 2, STAY)]
    rest_cols = gather_pairs(rest, [far,beyond], [sent[0]])
    (rest_fold,) = fold(away, rest_cols, BF16, joined=first_folds[1:])
    sent.append(hop(rest_fold, 2, STAY))
    home_near, home_near_sib = turn(
        [pieces[5]] + [hop(p, 0, c) for p, c in zip(pieces[6:9], chips)]
    )
    home_far, home_far_sib = turn(
        [beyond] + [hop(beyond[i + 1], 0, c) for i, c in enumerate(chips)]
    )
    home = [home_near, home_far, hop(home_near_sib, 0, SIBLING), hop(home_far_sib, 0, SIBLING)]
    folds = [fold(home, cols, F32)[0] for cols in (first_cols, rest_cols)]
    total = jnp.concatenate(folds, axis=1) + jnp.concatenate(sent, axis=1).astype(F32)
    return grad_query[None], grad_kv[None], total


def shards(normed_input, queries, keys_values, grad_output, doc_lengths):
    ctx = lax.axis_size("ctx")
    own = lax.axis_index("ctx")
    shard_rows, model_width = normed_input.shape[1:]
    grad_query, lead, terms, held = attention(
        own[None], doc_lengths, queries[0], grad_output[0], keys_values[0], cube=False
    )
    span = terms.shape[0]
    moved = [shift(terms[span - 1 - d], -d) for d in range(1, span)]
    rest, grad_kv = settle(grad_query, lead, held, moved)
    grad_cols = jnp.concatenate([lead, rest], axis=1)
    part = model_width // ctx
    pieces = normed_input[0].reshape(shard_rows, ctx, part)
    my_features = lax.all_to_all(pieces, "ctx", split_axis=1, concat_axis=0, tiled=True)
    my_features = my_features.reshape(ctx * shard_rows, part)
    partial = fold_rows(my_features, lax.all_gather(grad_cols, "ctx", axis=0, tiled=True))
    grad_weights = lax.psum_scatter(
        partial.astype(BF16), "dp", scatter_dimension=0, tiled=True
    ).astype(F32)
    return grad_query[None], grad_kv[None], grad_weights


def solution(mesh):
    cube = mesh.shape["dp"] == 4 and mesh.shape["ctx"] == 8
    spec = P("dp", "ctx", None)
    return jax.shard_map(
        shards_cube if cube else shards,
        mesh=mesh,
        in_specs=(spec, spec, spec, spec, P("dp", None)),
        out_specs=(spec, spec, P(("ctx", "dp"), None)),
        check_vma=False,
    )
```

```python
import functools

import jax
import jax.numpy as jnp
from jax import lax
from jax.experimental import pallas as pl
from jax.experimental.pallas import tpu as pltpu
from jax.sharding import PartitionSpec as P

F32 = jnp.float32
BF16 = jnp.bfloat16
VMEM_LIMIT = 16 * 1024 * 1024
LEAD = 4


def dot(a, b, ca, cb):
    return lax.dot_general(a, b, (((ca,), (cb,)), ((), ())), preferred_element_type=F32)


def attention_kernel(own_ref, lens_ref, q_ref, do_ref, *refs, span, head, group, docs, cube):
    kv_refs, (gq_ref, lead_ref), term_refs = refs[:span], refs[span : span + 2], refs[span + 2 :]
    rows = q_ref.shape[0]
    scale = head ** (-0.5)
    own = own_ref[0]
    first = jnp.int32(0)
    start = jnp.int32(0)
    for d in range(docs):
        first = jnp.where(start <= own, jnp.maximum(first, start), first)
        start = start + lens_ref[0, d]
    kv = jnp.concatenate([r[...] for r in kv_refs], axis=0)
    keys, values = kv[:, :head], kv[:, head:]
    keys_t = keys.T
    width = 2 * rows
    key_at = lax.broadcasted_iota(jnp.int32, (span * rows, width), 0)
    query_at = lax.broadcasted_iota(jnp.int32, (span * rows, width), 1) % rows
    low = (first - own + span - 1) * rows
    allowed = (key_at >= low) & (key_at <= query_at + (span - 1) * rows)
    dk = jnp.zeros((span * rows, head), F32)
    dv = jnp.zeros((span * rows, head), F32)
    for pair in range(group // 2):
        at = [2 * pair * head, (2 * pair + 1) * head]
        q2 = jnp.concatenate([q_ref[:, a : a + head] for a in at], axis=0)
        do2 = jnp.concatenate([do_ref[:, a : a + head] for a in at], axis=0)
        scores = jnp.where(allowed, dot(keys, q2, 1, 1) * scale, -1e30)
        exps = jnp.exp(scores - jnp.max(scores, axis=0, keepdims=True))
        probs = exps * (1.0 / jnp.sum(exps, axis=0, keepdims=True))
        probs_half = probs.astype(BF16)
        dprobs = dot(values, do2, 1, 1)
        row_dots = jnp.sum(probs_half.astype(F32) * dprobs, axis=0, keepdims=True)
        dscores_half = (probs * (dprobs - row_dots)).astype(BF16)
        dk = dk + dot(dscores_half, q2, 1, 0)
        dv = dv + dot(probs_half, do2, 1, 0)
        gq_t = dot(keys_t, dscores_half, 1, 0) * scale
        for i, a in enumerate(at):
            gq = gq_t[:, i * rows : (i + 1) * rows].T.astype(BF16)
            gq_ref[:, a : a + head] = gq
            if a < lead_ref.shape[1]:
                lead_ref[:, a : a + head] = gq
    terms = jnp.concatenate([dk * scale, dv], axis=1).astype(BF16).reshape(span, rows, 2 * head)
    if not cube:
        term_refs[0][...] = terms
        term_refs[1][...] = terms[span - 1]
        return
    for ref in term_refs:
        ref[...] = jnp.zeros_like(ref)
    for t in range(span):
        p = cube_place(own, own - (span - 1) + t)
        shown = own >= span - 1 - t

        for chip, ref in enumerate(term_refs):

            @pl.when(shown & (p // 2 == chip))
            def _(t=t, p=p, ref=ref):
                ref[p % 2] = terms[t].astype(ref.dtype)


def cube_place(own, shard):
    gap = jnp.bitwise_xor(own, shard % 8)
    core, across, along = gap % 2, gap // 2 % 2, gap // 4
    first = jnp.where(own % 2 == 0, across, along)
    return core + 2 * first + 4 * (across + along - first)


def shift(value, by):
    ctx = lax.axis_size("ctx")
    return lax.ppermute(value, "ctx", [(i, (i + by) % ctx) for i in range(ctx)])


def attention(own, lens, q, do, own_kv, cube):
    ctx = lax.axis_size("ctx")
    span = ctx // 2 + 1
    slots = [shift(own_kv, d) for d in range(span - 1, 0, -1)] + [own_kv]
    head = own_kv.shape[1] // 2
    rows = q.shape[0]
    group = q.shape[1] // head
    smem = pl.BlockSpec(memory_space=pltpu.SMEM)
    vmem = pl.BlockSpec(memory_space=pltpu.VMEM)
    if cube:
        terms = [jax.ShapeDtypeStruct((2, rows, 2 * head), t) for t in (F32, BF16, BF16, BF16)]
    else:
        terms = [jax.ShapeDtypeStruct(n + (rows, 2 * head), BF16) for n in ((span,), ())]
    return pl.pallas_call(
        functools.partial(
            attention_kernel, span=span, head=head, group=group, docs=lens.shape[1], cube=cube
        ),
        out_shape=(
            jax.ShapeDtypeStruct(q.shape, BF16),
            jax.ShapeDtypeStruct((rows, LEAD * head), BF16),
            *terms,
        ),
        in_specs=[smem, smem] + [vmem] * (2 + len(slots)),
        out_specs=(vmem,) * (2 + len(terms)),
        compiler_params=pltpu.CompilerParams(vmem_limit_bytes=VMEM_LIMIT),
        cost_estimate=pl.CostEstimate(
            flops=12 * group * rows * rows * span * head,
            bytes_accessed=6 * q.size + 4 * span * rows * 2 * head,
            transcendentals=group * rows * rows * span,
        ),
        name="attention",
    )(own, lens, q, do, *slots)


def spread_kernel(place_ref, x_ref, *outs, dp, part):
    z, c = place_ref[0], place_ref[1]
    first = 2 + 2 * (c % 2)
    for home in range(2):
        for far in range(2):
            for at, flip in enumerate((0, first, 6 - first, 6)):
                if home:
                    out = outs[9].at[at] if far else outs[5 + at]
                else:
                    out = outs[4].at[at] if far else outs[at]
                plane = z ^ far ^ (2 - 2 * home)
                for other in range(2):
                    src = pl.multiple_of(((c ^ flip ^ other) * dp + plane) * part, part)
                    out[other] = x_ref[:, pl.ds(src, part)]


def spread(place, x, ctx, dp):
    rows, width = x.shape
    part = width // (ctx * dp)
    piece = (2, rows, part)
    vmem = pl.BlockSpec(memory_space=pltpu.VMEM)
    shapes = ([piece] * 4 + [(4,) + piece]) * 2
    return pl.pallas_call(
        functools.partial(spread_kernel, dp=dp, part=part),
        out_shape=[jax.ShapeDtypeStruct(p, BF16) for p in shapes],
        in_specs=[pl.BlockSpec(memory_space=pltpu.SMEM), vmem],
        out_specs=[vmem] * len(shapes),
        compiler_params=pltpu.CompilerParams(vmem_limit_bytes=VMEM_LIMIT),
        cost_estimate=pl.CostEstimate(flops=0, bytes_accessed=4 * x.size, transcendentals=0),
        name="spread",
    )(place, x)


def local_call(kernel, name, out_shape, args, gates=(), smem=0, flops=0):
    vmem = pl.BlockSpec(memory_space=pltpu.VMEM)
    specs = [pl.BlockSpec(memory_space=pltpu.SMEM)] * smem + [vmem] * (len(args) - smem)
    specs += [pl.BlockSpec(memory_space=pl.ANY)] * len(gates)
    return pl.pallas_call(
        kernel,
        out_shape=out_shape,
        in_specs=specs,
        out_specs=jax.tree.map(lambda _: vmem, out_shape),
        compiler_params=pltpu.CompilerParams(vmem_limit_bytes=VMEM_LIMIT),
        cost_estimate=pl.CostEstimate(
            flops=flops,
            bytes_accessed=0,
            transcendentals=0,
        ),
        name=name,
    )(*args, *gates)


def turn_kernel(*refs):
    pieces, outs = refs[:4], refs[-2:]
    rows = pieces[1].shape[1]
    for at, piece in enumerate(pieces):
        piece = piece.at[0] if len(piece.shape) == 4 else piece
        for core in range(2):
            outs[core][:, at * rows : (at + 1) * rows] = piece[core].T


def turn(pieces, gates=()):
    _, rows, width = pieces[1].shape
    turned = jax.ShapeDtypeStruct((width, 4 * rows), BF16)
    return local_call(turn_kernel, "turn", (turned, turned), pieces, gates)


def pack_kernel(own_ref, moved_ref, *refs):
    n = own_ref.shape[0]
    refs[-1][:n] = own_ref[...]
    refs[-1][n:] = moved_ref[...]


def pack(own, moved, gates=()):
    out = jax.ShapeDtypeStruct((2 * own.shape[0],) + own.shape[1:], BF16)
    return local_call(pack_kernel, "pack", (out,), [own, moved], gates)[0]


def hold_kernel(*refs, count):
    for own, out in zip(refs[:count], refs[-count:]):
        out[...] = own[...]


def hold(own, gates):
    outs = [jax.ShapeDtypeStruct(a.shape, a.dtype) for a in own]
    kernel = functools.partial(hold_kernel, count=len(own))
    return local_call(kernel, "hold", outs, own, gates)


def merge_kernel(held_ref, *refs):
    moved, (hold_ref, send_ref) = refs[:3], refs[-2:]
    total = held_ref[...]
    for ref in moved:
        total = total + ref[...].astype(F32)
    hold_ref[...] = total[0]
    send_ref[...] = total[1].astype(BF16)


def merge(held, moved, gates=()):
    outs = tuple(jax.ShapeDtypeStruct(held.shape[1:], t) for t in (F32, BF16))
    return local_call(merge_kernel, "merge", outs, [held, *moved], gates)


def settle_kernel(gq_ref, held_ref, *refs):
    moved, (cols_ref, gkv_ref) = refs[:-2], refs[-2:]
    width = cols_ref.shape[1] - gkv_ref.shape[1]
    total = held_ref[...].astype(F32)
    for ref in moved:
        total = total + ref[...].astype(F32)
    gkv = total.astype(BF16)
    gkv_ref[...] = gkv
    cols_ref[:, :width] = gq_ref[:, gq_ref.shape[1] - width :]
    cols_ref[:, width:] = gkv


def settle(gq, lead, held, moved):
    rows, kv_width = held.shape
    outs = (
        jax.ShapeDtypeStruct((rows, gq.shape[1] - lead.shape[1] + kv_width), BF16),
        jax.ShapeDtypeStruct((rows, kv_width), BF16),
    )
    return local_call(settle_kernel, "settle", outs, [gq, held, *moved])


def fold_kernel(*refs, outs, joined):
    turned, cols, outs = refs[:4], refs[4:10], refs[-outs:]
    lead = refs[10] if joined else None
    rows = cols[0].shape[1]
    pairs = [(col, at) for col in cols for at in range(0, col.shape[0], 2)]
    total = None
    for core in range(2):
        for chip in range(4):
            span = slice(chip * rows, (chip + 1) * rows)
            left = jnp.concatenate([t[:, span] for t in turned[2 * core : 2 * core + 2]], axis=1)
            col, pair = pairs[4 * core + chip]
            term = dot(left, col[pair : pair + 2].reshape(2 * rows, col.shape[2]), 1, 0)
            total = term if total is None else total + term
    total = total.astype(outs[0].dtype)
    if joined:
        total = jnp.concatenate([lead[...], total], axis=1)
    start = 0
    for out in outs:
        out[...] = total[:, start : start + out.shape[1]]
        start += out.shape[1]


def fold(turned, cols, dtype, cuts=(), joined=()):
    half, depth = turned[0].shape
    n = cols[0].shape[2] + sum(j.shape[1] for j in joined)
    edges = [0, *cuts, n]
    outs = [jax.ShapeDtypeStruct((half, b - a), dtype) for a, b in zip(edges, edges[1:])]
    kernel = functools.partial(fold_kernel, outs=len(outs), joined=bool(joined))
    return local_call(kernel, "fold", outs, [*turned, *cols, *joined])


def fold_rows(features, piece_rows):
    return lax.dot_general(
        features, piece_rows, (((0,), (0,)), ((), ())), preferred_element_type=F32
    )


def hop(value, dz, of_core):
    pairs = [
        (8 * z + c, 8 * (z ^ dz) + (c ^ of_core[c % 2])) for z in range(4) for c in range(8)
    ]
    return lax.ppermute(value, ("dp", "ctx"), pairs)


FIRST, SECOND, DIAGONAL, STAY, SIBLING = (2, 4), (4, 2), (6, 6), (0, 0), (1, 1)


def gather_pairs(cols, gates, late_gates=()):
    both = pack(cols[None], hop(cols, 1, STAY)[None], gates)
    from_first = hop(both, 0, FIRST)
    from_second = hop(both, 0, SECOND)
    from_diagonal = hop(from_first, 0, SECOND)
    near = hop(pack(both, from_first), 0, SIBLING)
    far = hop(pack(from_second, from_diagonal, late_gates), 0, SIBLING)
    return [both, from_first, from_second, from_diagonal, near, far]


def shards_cube(normed_input, queries, keys_values, grad_output, doc_lengths):
    ctx, dp = lax.axis_size("ctx"), lax.axis_size("dp")
    own, z = lax.axis_index("ctx"), lax.axis_index("dp")
    pieces = spread(jnp.stack([z, own]), normed_input[0], ctx, dp)
    grad_query, lead, held, *send = attention(
        own[None], doc_lengths, queries[0], grad_output[0], keys_values[0], cube=True
    )
    chips = (FIRST, SECOND, DIAGONAL)
    near, near_sib = turn([pieces[0]] + [hop(p, 0, c) for p, c in zip(pieces[1:4], chips)])
    across = hop(pieces[4], 1, STAY)
    far, far_sib = turn([across] + [hop(across[i + 1], 0, c) for i, c in enumerate(chips)])
    away = [near, far, hop(near_sib, 0, SIBLING), hop(far_sib, 0, SIBLING)]
    first_cols = gather_pairs(lead, [near])
    beyond = hop(hold([pieces[9]], [first_cols[0]])[0], 1, STAY)
    held, send = merge(held, [hop(t, 0, c) for t, c in zip(send, chips)])
    rest, grad_kv = settle(grad_query, lead, held, [hop(send, 0, SIBLING)])
    first_folds = fold(away, first_cols, BF16, cuts=[384])
    sent = [hop(first_folds[0], 2, STAY)]
    rest_cols = gather_pairs(rest, [far,beyond], [sent[0]])
    (rest_fold,) = fold(away, rest_cols, BF16, joined=first_folds[1:])
    sent.append(hop(rest_fold, 2, STAY))
    held_pieces = hold(pieces[6:9], [rest_fold])
    home_near, home_near_sib = turn(
        [pieces[5]] + [hop(p, 0, c) for p, c in zip(held_pieces, chips)]
    )
    home_far, home_far_sib = turn(
        [beyond] + [hop(beyond[i + 1], 0, c) for i, c in enumerate(chips)]
    )
    home = [home_near, home_far, hop(home_near_sib, 0, SIBLING), hop(home_far_sib, 0, SIBLING)]
    folds = [fold(home, cols, F32)[0] for cols in (first_cols, rest_cols)]
    total = jnp.concatenate(folds, axis=1) + jnp.concatenate(sent, axis=1).astype(F32)
    return grad_query[None], grad_kv[None], total


def shards(normed_input, queries, keys_values, grad_output, doc_lengths):
    ctx = lax.axis_size("ctx")
    own = lax.axis_index("ctx")
    shard_rows, model_width = normed_input.shape[1:]
    grad_query, lead, terms, held = attention(
        own[None], doc_lengths, queries[0], grad_output[0], keys_values[0], cube=False
    )
    span = terms.shape[0]
    moved = [shift(terms[span - 1 - d], -d) for d in range(1, span)]
    rest, grad_kv = settle(grad_query, lead, held, moved)
    grad_cols = jnp.concatenate([lead, rest], axis=1)
    part = model_width // ctx
    pieces = normed_input[0].reshape(shard_rows, ctx, part)
    my_features = lax.all_to_all(pieces, "ctx", split_axis=1, concat_axis=0, tiled=True)
    my_features = my_features.reshape(ctx * shard_rows, part)
    partial = fold_rows(my_features, lax.all_gather(grad_cols, "ctx", axis=0, tiled=True))
    grad_weights = lax.psum_scatter(
        partial.astype(BF16), "dp", scatter_dimension=0, tiled=True
    ).astype(F32)
    return grad_query[None], grad_kv[None], grad_weights


def solution(mesh):
    cube = mesh.shape["dp"] == 4 and mesh.shape["ctx"] == 8
    spec = P("dp", "ctx", None)
    return jax.shard_map(
        shards_cube if cube else shards,
        mesh=mesh,
        in_specs=(spec, spec, spec, spec, P("dp", None)),
        out_specs=(spec, spec, P(("ctx", "dp"), None)),
        check_vma=False,
    )
```

```python
import functools

import jax
import jax.numpy as jnp
from jax import lax
from jax.experimental import pallas as pl
from jax.experimental.pallas import tpu as pltpu
from jax.sharding import PartitionSpec as P

F32 = jnp.float32
BF16 = jnp.bfloat16
VMEM_LIMIT = 16 * 1024 * 1024
LEAD = 4


def dot(a, b, ca, cb):
    return lax.dot_general(a, b, (((ca,), (cb,)), ((), ())), preferred_element_type=F32)


def attention_kernel(own_ref, lens_ref, q_ref, do_ref, *refs, span, head, group, docs, cube):
    kv_refs, (gq_ref, lead_ref), term_refs = refs[:span], refs[span : span + 2], refs[span + 2 :]
    rows = q_ref.shape[0]
    scale = head ** (-0.5)
    own = own_ref[0]
    first = jnp.int32(0)
    start = jnp.int32(0)
    for d in range(docs):
        first = jnp.where(start <= own, jnp.maximum(first, start), first)
        start = start + lens_ref[0, d]
    kv = jnp.concatenate([r[...] for r in kv_refs], axis=0)
    keys, values = kv[:, :head], kv[:, head:]
    keys_t = keys.T
    width = 2 * rows
    key_at = lax.broadcasted_iota(jnp.int32, (span * rows, width), 0)
    query_at = lax.broadcasted_iota(jnp.int32, (span * rows, width), 1) % rows
    low = (first - own + span - 1) * rows
    allowed = (key_at >= low) & (key_at <= query_at + (span - 1) * rows)
    dk = jnp.zeros((span * rows, head), F32)
    dv = jnp.zeros((span * rows, head), F32)
    for pair in range(group // 2):
        at = [2 * pair * head, (2 * pair + 1) * head]
        q2 = jnp.concatenate([q_ref[:, a : a + head] for a in at], axis=0)
        do2 = jnp.concatenate([do_ref[:, a : a + head] for a in at], axis=0)
        scores = jnp.where(allowed, dot(keys, q2, 1, 1) * scale, -1e30)
        exps = jnp.exp(scores - jnp.max(scores, axis=0, keepdims=True))
        probs = exps * (1.0 / jnp.sum(exps, axis=0, keepdims=True))
        probs_half = probs.astype(BF16)
        dprobs = dot(values, do2, 1, 1)
        row_dots = jnp.sum(probs_half.astype(F32) * dprobs, axis=0, keepdims=True)
        dscores_half = (probs * (dprobs - row_dots)).astype(BF16)
        dk = dk + dot(dscores_half, q2, 1, 0)
        dv = dv + dot(probs_half, do2, 1, 0)
        gq_t = dot(keys_t, dscores_half, 1, 0) * scale
        for i, a in enumerate(at):
            gq = gq_t[:, i * rows : (i + 1) * rows].T.astype(BF16)
            gq_ref[:, a : a + head] = gq
            if a < lead_ref.shape[1]:
                lead_ref[:, a : a + head] = gq
    terms = jnp.concatenate([dk * scale, dv], axis=1).astype(BF16).reshape(span, rows, 2 * head)
    if not cube:
        term_refs[0][...] = terms
        term_refs[1][...] = terms[span - 1]
        return
    for ref in term_refs:
        ref[...] = jnp.zeros_like(ref)
    for t in range(span):
        p = cube_place(own, own - (span - 1) + t)
        shown = own >= span - 1 - t

        for chip, ref in enumerate(term_refs):

            @pl.when(shown & (p // 2 == chip))
            def _(t=t, p=p, ref=ref):
                ref[p % 2] = terms[t].astype(ref.dtype)


def cube_place(own, shard):
    gap = jnp.bitwise_xor(own, shard % 8)
    core, across, along = gap % 2, gap // 2 % 2, gap // 4
    first = jnp.where(own % 2 == 0, across, along)
    return core + 2 * first + 4 * (across + along - first)


def shift(value, by):
    ctx = lax.axis_size("ctx")
    return lax.ppermute(value, "ctx", [(i, (i + by) % ctx) for i in range(ctx)])


def attention(own, lens, q, do, own_kv, cube):
    ctx = lax.axis_size("ctx")
    span = ctx // 2 + 1
    slots = [shift(own_kv, d) for d in range(span - 1, 0, -1)] + [own_kv]
    head = own_kv.shape[1] // 2
    rows = q.shape[0]
    group = q.shape[1] // head
    smem = pl.BlockSpec(memory_space=pltpu.SMEM)
    vmem = pl.BlockSpec(memory_space=pltpu.VMEM)
    if cube:
        terms = [jax.ShapeDtypeStruct((2, rows, 2 * head), t) for t in (F32, BF16, BF16, BF16)]
    else:
        terms = [jax.ShapeDtypeStruct(n + (rows, 2 * head), BF16) for n in ((span,), ())]
    return pl.pallas_call(
        functools.partial(
            attention_kernel, span=span, head=head, group=group, docs=lens.shape[1], cube=cube
        ),
        out_shape=(
            jax.ShapeDtypeStruct(q.shape, BF16),
            jax.ShapeDtypeStruct((rows, LEAD * head), BF16),
            *terms,
        ),
        in_specs=[smem, smem] + [vmem] * (2 + len(slots)),
        out_specs=(vmem,) * (2 + len(terms)),
        compiler_params=pltpu.CompilerParams(vmem_limit_bytes=VMEM_LIMIT),
        cost_estimate=pl.CostEstimate(
            flops=12 * group * rows * rows * span * head,
            bytes_accessed=6 * q.size + 4 * span * rows * 2 * head,
            transcendentals=group * rows * rows * span,
        ),
        name="attention",
    )(own, lens, q, do, *slots)


def spread_kernel(place_ref, x_ref, *outs, dp, part):
    z, c = place_ref[0], place_ref[1]
    first = 2 + 2 * (c % 2)
    for home in range(2):
        for far in range(2):
            for at, flip in enumerate((0, first, 6 - first, 6)):
                if home:
                    out = outs[9].at[at] if far else outs[5 + at]
                else:
                    out = outs[4].at[at] if far else outs[at]
                plane = z ^ far ^ (2 - 2 * home)
                for other in range(2):
                    src = pl.multiple_of(((c ^ flip ^ other) * dp + plane) * part, part)
                    out[other] = x_ref[:, pl.ds(src, part)]


def spread(place, x, ctx, dp):
    rows, width = x.shape
    part = width // (ctx * dp)
    piece = (2, rows, part)
    vmem = pl.BlockSpec(memory_space=pltpu.VMEM)
    shapes = ([piece] * 4 + [(4,) + piece]) * 2
    return pl.pallas_call(
        functools.partial(spread_kernel, dp=dp, part=part),
        out_shape=[jax.ShapeDtypeStruct(p, BF16) for p in shapes],
        in_specs=[pl.BlockSpec(memory_space=pltpu.SMEM), vmem],
        out_specs=[vmem] * len(shapes),
        compiler_params=pltpu.CompilerParams(vmem_limit_bytes=VMEM_LIMIT),
        cost_estimate=pl.CostEstimate(flops=0, bytes_accessed=4 * x.size, transcendentals=0),
        name="spread",
    )(place, x)


def local_call(kernel, name, out_shape, args, gates=(), smem=0, flops=0):
    vmem = pl.BlockSpec(memory_space=pltpu.VMEM)
    specs = [pl.BlockSpec(memory_space=pltpu.SMEM)] * smem + [vmem] * (len(args) - smem)
    specs += [pl.BlockSpec(memory_space=pl.ANY)] * len(gates)
    return pl.pallas_call(
        kernel,
        out_shape=out_shape,
        in_specs=specs,
        out_specs=jax.tree.map(lambda _: vmem, out_shape),
        compiler_params=pltpu.CompilerParams(vmem_limit_bytes=VMEM_LIMIT),
        cost_estimate=pl.CostEstimate(
            flops=flops,
            bytes_accessed=0,
            transcendentals=0,
        ),
        name=name,
    )(*args, *gates)


def turn_kernel(*refs):
    pieces, outs = refs[:4], refs[-2:]
    rows = pieces[1].shape[1]
    for at, piece in enumerate(pieces):
        piece = piece.at[0] if len(piece.shape) == 4 else piece
        for core in range(2):
            outs[core][:, at * rows : (at + 1) * rows] = piece[core].T


def turn(pieces, gates=()):
    _, rows, width = pieces[1].shape
    turned = jax.ShapeDtypeStruct((width, 4 * rows), BF16)
    return local_call(turn_kernel, "turn", (turned, turned), pieces, gates)


def pack_kernel(own_ref, moved_ref, *refs):
    n = own_ref.shape[0]
    refs[-1][:n] = own_ref[...]
    refs[-1][n:] = moved_ref[...]


def pack(own, moved, gates=()):
    out = jax.ShapeDtypeStruct((2 * own.shape[0],) + own.shape[1:], BF16)
    return local_call(pack_kernel, "pack", (out,), [own, moved], gates)[0]


def hold_kernel(*refs, count):
    for own, out in zip(refs[:count], refs[-count:]):
        out[...] = own[...]


def hold(own, gates):
    outs = [jax.ShapeDtypeStruct(a.shape, a.dtype) for a in own]
    kernel = functools.partial(hold_kernel, count=len(own))
    return local_call(kernel, "hold", outs, own, gates)


def merge_kernel(held_ref, *refs):
    moved, (hold_ref, send_ref) = refs[:3], refs[-2:]
    total = held_ref[...]
    for ref in moved:
        total = total + ref[...].astype(F32)
    hold_ref[...] = total[0]
    send_ref[...] = total[1].astype(BF16)


def merge(held, moved, gates=()):
    outs = tuple(jax.ShapeDtypeStruct(held.shape[1:], t) for t in (F32, BF16))
    return local_call(merge_kernel, "merge", outs, [held, *moved], gates)


def settle_kernel(gq_ref, held_ref, *refs):
    moved, (cols_ref, gkv_ref) = refs[:-2], refs[-2:]
    width = cols_ref.shape[1] - gkv_ref.shape[1]
    total = held_ref[...].astype(F32)
    for ref in moved:
        total = total + ref[...].astype(F32)
    gkv = total.astype(BF16)
    gkv_ref[...] = gkv
    cols_ref[:, :width] = gq_ref[:, gq_ref.shape[1] - width :]
    cols_ref[:, width:] = gkv


def settle(gq, lead, held, moved):
    rows, kv_width = held.shape
    outs = (
        jax.ShapeDtypeStruct((rows, gq.shape[1] - lead.shape[1] + kv_width), BF16),
        jax.ShapeDtypeStruct((rows, kv_width), BF16),
    )
    return local_call(settle_kernel, "settle", outs, [gq, held, *moved])


def fold_kernel(*refs, outs, joined):
    turned, cols, outs = refs[:4], refs[4:10], refs[-outs:]
    lead = refs[10] if joined else None
    rows = cols[0].shape[1]
    pairs = [(col, at) for col in cols for at in range(0, col.shape[0], 2)]
    total = None
    for core in range(2):
        for chip in range(4):
            span = slice(chip * rows, (chip + 1) * rows)
            left = jnp.concatenate([t[:, span] for t in turned[2 * core : 2 * core + 2]], axis=1)
            col, pair = pairs[4 * core + chip]
            term = dot(left, col[pair : pair + 2].reshape(2 * rows, col.shape[2]), 1, 0)
            total = term if total is None else total + term
    total = total.astype(outs[0].dtype)
    if joined:
        total = jnp.concatenate([lead[...], total], axis=1)
    start = 0
    for out in outs:
        out[...] = total[:, start : start + out.shape[1]]
        start += out.shape[1]


def fold(turned, cols, dtype, cuts=(), joined=()):
    half, depth = turned[0].shape
    n = cols[0].shape[2] + sum(j.shape[1] for j in joined)
    edges = [0, *cuts, n]
    outs = [jax.ShapeDtypeStruct((half, b - a), dtype) for a, b in zip(edges, edges[1:])]
    kernel = functools.partial(fold_kernel, outs=len(outs), joined=bool(joined))
    return local_call(kernel, "fold", outs, [*turned, *cols, *joined])


def fold_rows(features, piece_rows):
    return lax.dot_general(
        features, piece_rows, (((0,), (0,)), ((), ())), preferred_element_type=F32
    )


def hop(value, dz, of_core):
    pairs = [
        (8 * z + c, 8 * (z ^ dz) + (c ^ of_core[c % 2])) for z in range(4) for c in range(8)
    ]
    return lax.ppermute(value, ("dp", "ctx"), pairs)


FIRST, SECOND, DIAGONAL, STAY, SIBLING = (2, 4), (4, 2), (6, 6), (0, 0), (1, 1)


def gather_pairs(cols, gates, late_gates=()):
    both = pack(cols[None], hop(cols, 1, STAY)[None], gates)
    from_first = hop(both, 0, FIRST)
    from_second = hop(both, 0, SECOND)
    from_diagonal = hop(from_first, 0, SECOND)
    near = hop(pack(both, from_first), 0, SIBLING)
    far = hop(pack(from_second, from_diagonal, late_gates), 0, SIBLING)
    return [both, from_first, from_second, from_diagonal, near, far]


def shards_cube(normed_input, queries, keys_values, grad_output, doc_lengths):
    ctx, dp = lax.axis_size("ctx"), lax.axis_size("dp")
    own, z = lax.axis_index("ctx"), lax.axis_index("dp")
    pieces = spread(jnp.stack([z, own]), normed_input[0], ctx, dp)
    grad_query, lead, held, *send = attention(
        own[None], doc_lengths, queries[0], grad_output[0], keys_values[0], cube=True
    )
    chips = (FIRST, SECOND, DIAGONAL)
    near, near_sib = turn([pieces[0]] + [hop(p, 0, c) for p, c in zip(pieces[1:4], chips)])
    across = hop(pieces[4], 1, STAY)
    far, far_sib = turn([across] + [hop(across[i + 1], 0, c) for i, c in enumerate(chips)])
    away = [near, far, hop(near_sib, 0, SIBLING), hop(far_sib, 0, SIBLING)]
    first_cols = gather_pairs(lead, [near])
    beyond = hop(hold([pieces[9]], [near])[0], 1, STAY)
    held, send = merge(held, [hop(t, 0, c) for t, c in zip(send, chips)])
    rest, grad_kv = settle(grad_query, lead, held, [hop(send, 0, SIBLING)])
    first_folds = fold(away, first_cols, BF16, cuts=[384])
    sent = [hop(first_folds[0], 2, STAY)]
    rest_cols = gather_pairs(rest, [far,beyond], [sent[0]])
    (rest_fold,) = fold(away, rest_cols, BF16, joined=first_folds[1:])
    sent.append(hop(rest_fold, 2, STAY))
    held_pieces = hold(pieces[6:9], [rest_fold])
    home_near, home_near_sib = turn(
        [pieces[5]] + [hop(p, 0, c) for p, c in zip(held_pieces, chips)]
    )
    home_far, home_far_sib = turn(
        [beyond] + [hop(beyond[i + 1], 0, c) for i, c in enumerate(chips)]
    )
    home = [home_near, home_far, hop(home_near_sib, 0, SIBLING), hop(home_far_sib, 0, SIBLING)]
    folds = [fold(home, cols, F32)[0] for cols in (first_cols, rest_cols)]
    total = jnp.concatenate(folds, axis=1) + jnp.concatenate(sent, axis=1).astype(F32)
    return grad_query[None], grad_kv[None], total


def shards(normed_input, queries, keys_values, grad_output, doc_lengths):
    ctx = lax.axis_size("ctx")
    own = lax.axis_index("ctx")
    shard_rows, model_width = normed_input.shape[1:]
    grad_query, lead, terms, held = attention(
        own[None], doc_lengths, queries[0], grad_output[0], keys_values[0], cube=False
    )
    span = terms.shape[0]
    moved = [shift(terms[span - 1 - d], -d) for d in range(1, span)]
    rest, grad_kv = settle(grad_query, lead, held, moved)
    grad_cols = jnp.concatenate([lead, rest], axis=1)
    part = model_width // ctx
    pieces = normed_input[0].reshape(shard_rows, ctx, part)
    my_features = lax.all_to_all(pieces, "ctx", split_axis=1, concat_axis=0, tiled=True)
    my_features = my_features.reshape(ctx * shard_rows, part)
    partial = fold_rows(my_features, lax.all_gather(grad_cols, "ctx", axis=0, tiled=True))
    grad_weights = lax.psum_scatter(
        partial.astype(BF16), "dp", scatter_dimension=0, tiled=True
    ).astype(F32)
    return grad_query[None], grad_kv[None], grad_weights


def solution(mesh):
    cube = mesh.shape["dp"] == 4 and mesh.shape["ctx"] == 8
    spec = P("dp", "ctx", None)
    return jax.shard_map(
        shards_cube if cube else shards,
        mesh=mesh,
        in_specs=(spec, spec, spec, spec, P("dp", None)),
        out_specs=(spec, spec, P(("ctx", "dp"), None)),
        check_vma=False,
    )
```

```python
import functools

import jax
import jax.numpy as jnp
from jax import lax
from jax.experimental import pallas as pl
from jax.experimental.pallas import tpu as pltpu
from jax.sharding import PartitionSpec as P

F32 = jnp.float32
BF16 = jnp.bfloat16
VMEM_LIMIT = 16 * 1024 * 1024
LEAD = 4
LOG2_E = 1.4426950408889634


def dot(a, b, ca, cb):
    return lax.dot_general(a, b, (((ca,), (cb,)), ((), ())), preferred_element_type=F32)


def attention_kernel(own_ref, lens_ref, q_ref, do_ref, *refs, span, head, group, docs, cube):
    kv_refs, (gq_ref, lead_ref), term_refs = refs[:span], refs[span : span + 2], refs[span + 2 :]
    rows = q_ref.shape[0]
    scale = head ** (-0.5)
    own = own_ref[0]
    first = jnp.int32(0)
    start = jnp.int32(0)
    for d in range(docs):
        first = jnp.where(start <= own, jnp.maximum(first, start), first)
        start = start + lens_ref[0, d]
    kv = jnp.concatenate([r[...] for r in kv_refs], axis=0)
    keys, values = kv[:, :head], kv[:, head:]
    keys_t = keys.T
    width = 2 * rows
    key_at = lax.broadcasted_iota(jnp.int32, (span * rows, width), 0)
    query_at = lax.broadcasted_iota(jnp.int32, (span * rows, width), 1) % rows
    low = (first - own + span - 1) * rows
    last = (span - 1) * rows
    dk = jnp.zeros((span * rows, head), F32)
    dv = jnp.zeros((span * rows, head), F32)
    for pair in range(group // 2):
        at = [2 * pair * head, (2 * pair + 1) * head]
        q2 = jnp.concatenate([q_ref[:, a : a + head] for a in at], axis=0)
        do2 = jnp.concatenate([do_ref[:, a : a + head] for a in at], axis=0)
        scores = dot(keys, q2, 1, 1)
        scores = jnp.concatenate(
            [
                jnp.where(key_at[:last] >= low, scores[:last], -1e30),
                jnp.where(key_at[:rows] <= query_at[:rows], scores[last:], -1e30),
            ],
            axis=0,
        )
        exps = jnp.exp2((scores - jnp.max(scores, axis=0, keepdims=True)) * (scale * LOG2_E))
        inverse = 1.0 / jnp.sum(exps, axis=0, keepdims=True)
        probs = exps * inverse
        probs_half = probs.astype(BF16)
        dprobs = dot(values, do2, 1, 1)
        row_dots = jnp.sum(probs_half.astype(F32) * dprobs, axis=0, keepdims=True)
        dscores_half = (probs * (dprobs - row_dots)).astype(BF16)
        dk = dk + dot(dscores_half, q2, 1, 0)
        dv = dv + dot(probs_half, do2, 1, 0)
        gq_t = dot(keys_t, dscores_half, 1, 0) * scale
        for i, a in enumerate(at):
            gq = gq_t[:, i * rows : (i + 1) * rows].T.astype(BF16)
            gq_ref[:, a : a + head] = gq
            if a < lead_ref.shape[1]:
                lead_ref[:, a : a + head] = gq
    terms = jnp.concatenate([dk * scale, dv], axis=1).astype(BF16).reshape(span, rows, 2 * head)
    if not cube:
        term_refs[0][...] = terms
        term_refs[1][...] = terms[span - 1]
        return
    for ref in term_refs:
        ref[...] = jnp.zeros_like(ref)
    for t in range(span):
        p = cube_place(own, own - (span - 1) + t)
        shown = own >= span - 1 - t

        for chip, ref in enumerate(term_refs):

            @pl.when(shown & (p // 2 == chip))
            def _(t=t, p=p, ref=ref):
                ref[p % 2] = terms[t].astype(ref.dtype)


def cube_place(own, shard):
    gap = jnp.bitwise_xor(own, shard % 8)
    core, across, along = gap % 2, gap // 2 % 2, gap // 4
    first = jnp.where(own % 2 == 0, across, along)
    return core + 2 * first + 4 * (across + along - first)


def shift(value, by):
    ctx = lax.axis_size("ctx")
    return lax.ppermute(value, "ctx", [(i, (i + by) % ctx) for i in range(ctx)])


def attention(own, lens, q, do, own_kv, cube):
    ctx = lax.axis_size("ctx")
    span = ctx // 2 + 1
    slots = [shift(own_kv, d) for d in range(span - 1, 0, -1)] + [own_kv]
    head = own_kv.shape[1] // 2
    rows = q.shape[0]
    group = q.shape[1] // head
    smem = pl.BlockSpec(memory_space=pltpu.SMEM)
    vmem = pl.BlockSpec(memory_space=pltpu.VMEM)
    if cube:
        terms = [jax.ShapeDtypeStruct((2, rows, 2 * head), t) for t in (F32, BF16, BF16, BF16)]
    else:
        terms = [jax.ShapeDtypeStruct(n + (rows, 2 * head), BF16) for n in ((span,), ())]
    return pl.pallas_call(
        functools.partial(
            attention_kernel, span=span, head=head, group=group, docs=lens.shape[1], cube=cube
        ),
        out_shape=(
            jax.ShapeDtypeStruct(q.shape, BF16),
            jax.ShapeDtypeStruct((rows, LEAD * head), BF16),
            *terms,
        ),
        in_specs=[smem, smem] + [vmem] * (2 + len(slots)),
        out_specs=(vmem,) * (2 + len(terms)),
        compiler_params=pltpu.CompilerParams(vmem_limit_bytes=VMEM_LIMIT),
        cost_estimate=pl.CostEstimate(
            flops=12 * group * rows * rows * span * head,
            bytes_accessed=6 * q.size + 4 * span * rows * 2 * head,
            transcendentals=group * rows * rows * span,
        ),
        name="attention",
    )(own, lens, q, do, *slots)


def spread_kernel(place_ref, x_ref, *outs, dp, part):
    z, c = place_ref[0], place_ref[1]
    first = 2 + 2 * (c % 2)
    for home in range(2):
        for far in range(2):
            for at, flip in enumerate((0, first, 6 - first, 6)):
                if home:
                    out = outs[9].at[at] if far else outs[5 + at]
                else:
                    out = outs[4].at[at] if far else outs[at]
                plane = z ^ far ^ (2 - 2 * home)
                for other in range(2):
                    src = pl.multiple_of(((c ^ flip ^ other) * dp + plane) * part, part)
                    out[other] = x_ref[:, pl.ds(src, part)]


def spread(place, x, ctx, dp):
    rows, width = x.shape
    part = width // (ctx * dp)
    piece = (2, rows, part)
    vmem = pl.BlockSpec(memory_space=pltpu.VMEM)
    shapes = ([piece] * 4 + [(4,) + piece]) * 2
    return pl.pallas_call(
        functools.partial(spread_kernel, dp=dp, part=part),
        out_shape=[jax.ShapeDtypeStruct(p, BF16) for p in shapes],
        in_specs=[pl.BlockSpec(memory_space=pltpu.SMEM), vmem],
        out_specs=[vmem] * len(shapes),
        compiler_params=pltpu.CompilerParams(vmem_limit_bytes=VMEM_LIMIT),
        cost_estimate=pl.CostEstimate(flops=0, bytes_accessed=4 * x.size, transcendentals=0),
        name="spread",
    )(place, x)


def local_call(kernel, name, out_shape, args, gates=(), smem=0, flops=0):
    vmem = pl.BlockSpec(memory_space=pltpu.VMEM)
    specs = [pl.BlockSpec(memory_space=pltpu.SMEM)] * smem + [vmem] * (len(args) - smem)
    specs += [pl.BlockSpec(memory_space=pl.ANY)] * len(gates)
    return pl.pallas_call(
        kernel,
        out_shape=out_shape,
        in_specs=specs,
        out_specs=jax.tree.map(lambda _: vmem, out_shape),
        compiler_params=pltpu.CompilerParams(vmem_limit_bytes=VMEM_LIMIT),
        cost_estimate=pl.CostEstimate(
            flops=flops,
            bytes_accessed=0,
            transcendentals=0,
        ),
        name=name,
    )(*args, *gates)


def turn_kernel(*refs):
    pieces, outs = refs[:4], refs[-2:]
    rows = pieces[1].shape[1]
    for at, piece in enumerate(pieces):
        piece = piece.at[0] if len(piece.shape) == 4 else piece
        for core in range(2):
            outs[core][:, at * rows : (at + 1) * rows] = piece[core].T


def turn(pieces, gates=()):
    _, rows, width = pieces[1].shape
    turned = jax.ShapeDtypeStruct((width, 4 * rows), BF16)
    return local_call(turn_kernel, "turn", (turned, turned), pieces, gates)


def pack_kernel(own_ref, moved_ref, *refs):
    n = own_ref.shape[0]
    refs[-1][:n] = own_ref[...]
    refs[-1][n:] = moved_ref[...]


def pack(own, moved, gates=()):
    out = jax.ShapeDtypeStruct((2 * own.shape[0],) + own.shape[1:], BF16)
    return local_call(pack_kernel, "pack", (out,), [own, moved], gates)[0]


def hold_kernel(*refs, count):
    for own, out in zip(refs[:count], refs[-count:]):
        out[...] = own[...]


def hold(own, gates):
    outs = [jax.ShapeDtypeStruct(a.shape, a.dtype) for a in own]
    kernel = functools.partial(hold_kernel, count=len(own))
    return local_call(kernel, "hold", outs, own, gates)


def merge_kernel(held_ref, *refs):
    moved, (hold_ref, send_ref) = refs[:3], refs[-2:]
    total = held_ref[...]
    for ref in moved:
        total = total + ref[...].astype(F32)
    hold_ref[...] = total[0]
    send_ref[...] = total[1].astype(BF16)


def merge(held, moved, gates=()):
    outs = tuple(jax.ShapeDtypeStruct(held.shape[1:], t) for t in (F32, BF16))
    return local_call(merge_kernel, "merge", outs, [held, *moved], gates)


def settle_kernel(gq_ref, held_ref, *refs):
    moved, (cols_ref, gkv_ref) = refs[:-2], refs[-2:]
    width = cols_ref.shape[1] - gkv_ref.shape[1]
    total = held_ref[...].astype(F32)
    for ref in moved:
        total = total + ref[...].astype(F32)
    gkv = total.astype(BF16)
    gkv_ref[...] = gkv
    cols_ref[:, :width] = gq_ref[:, gq_ref.shape[1] - width :]
    cols_ref[:, width:] = gkv


def settle(gq, lead, held, moved):
    rows, kv_width = held.shape
    outs = (
        jax.ShapeDtypeStruct((rows, gq.shape[1] - lead.shape[1] + kv_width), BF16),
        jax.ShapeDtypeStruct((rows, kv_width), BF16),
    )
    return local_call(settle_kernel, "settle", outs, [gq, held, *moved])


def fold_kernel(*refs, outs, joined):
    turned, cols, outs = refs[:4], refs[4:10], refs[-outs:]
    lead = refs[10] if joined else None
    rows = cols[0].shape[1]
    pairs = [(col, at) for col in cols for at in range(0, col.shape[0], 2)]
    total = None
    for core in range(2):
        for chip in range(4):
            span = slice(chip * rows, (chip + 1) * rows)
            left = jnp.concatenate([t[:, span] for t in turned[2 * core : 2 * core + 2]], axis=1)
            col, pair = pairs[4 * core + chip]
            term = dot(left, col[pair : pair + 2].reshape(2 * rows, col.shape[2]), 1, 0)
            total = term if total is None else total + term
    total = total.astype(outs[0].dtype)
    if joined:
        total = jnp.concatenate([lead[...], total], axis=1)
    start = 0
    for out in outs:
        out[...] = total[:, start : start + out.shape[1]]
        start += out.shape[1]


def fold(turned, cols, dtype, cuts=(), joined=()):
    half, depth = turned[0].shape
    n = cols[0].shape[2] + sum(j.shape[1] for j in joined)
    edges = [0, *cuts, n]
    outs = [jax.ShapeDtypeStruct((half, b - a), dtype) for a, b in zip(edges, edges[1:])]
    kernel = functools.partial(fold_kernel, outs=len(outs), joined=bool(joined))
    return local_call(kernel, "fold", outs, [*turned, *cols, *joined])


def fold_rows(features, piece_rows):
    return lax.dot_general(
        features, piece_rows, (((0,), (0,)), ((), ())), preferred_element_type=F32
    )


def hop(value, dz, of_core):
    pairs = [
        (8 * z + c, 8 * (z ^ dz) + (c ^ of_core[c % 2])) for z in range(4) for c in range(8)
    ]
    return lax.ppermute(value, ("dp", "ctx"), pairs)


FIRST, SECOND, DIAGONAL, STAY, SIBLING = (2, 4), (4, 2), (6, 6), (0, 0), (1, 1)


def gather_pairs(cols, gates, late_gates=()):
    both = pack(cols[None], hop(cols, 1, STAY)[None], gates)
    from_first = hop(both, 0, FIRST)
    from_second = hop(both, 0, SECOND)
    from_diagonal = hop(from_first, 0, SECOND)
    near = hop(pack(both, from_first), 0, SIBLING)
    far = hop(pack(from_second, from_diagonal, late_gates), 0, SIBLING)
    return [both, from_first, from_second, from_diagonal, near, far]


def shards_cube(normed_input, queries, keys_values, grad_output, doc_lengths):
    ctx, dp = lax.axis_size("ctx"), lax.axis_size("dp")
    own, z = lax.axis_index("ctx"), lax.axis_index("dp")
    pieces = spread(jnp.stack([z, own]), normed_input[0], ctx, dp)
    grad_query, lead, held, *send = attention(
        own[None], doc_lengths, queries[0], grad_output[0], keys_values[0], cube=True
    )
    chips = (FIRST, SECOND, DIAGONAL)
    near, near_sib = turn([pieces[0]] + [hop(p, 0, c) for p, c in zip(pieces[1:4], chips)])
    across = hop(pieces[4], 1, STAY)
    far, far_sib = turn([across] + [hop(across[i + 1], 0, c) for i, c in enumerate(chips)])
    away = [near, far, hop(near_sib, 0, SIBLING), hop(far_sib, 0, SIBLING)]
    first_cols = gather_pairs(lead, [near])
    beyond = hop(hold([pieces[9]], [near])[0], 1, STAY)
    held, send = merge(held, [hop(t, 0, c) for t, c in zip(send, chips)])
    rest, grad_kv = settle(grad_query, lead, held, [hop(send, 0, SIBLING)])
    first_folds = fold(away, first_cols, BF16, cuts=[384])
    sent = [hop(first_folds[0], 2, STAY)]
    rest_cols = gather_pairs(rest, [far,beyond], [sent[0]])
    (rest_fold,) = fold(away, rest_cols, BF16, joined=first_folds[1:])
    sent.append(hop(rest_fold, 2, STAY))
    held_pieces = hold(pieces[6:9], [rest_fold])
    home_near, home_near_sib = turn(
        [pieces[5]] + [hop(p, 0, c) for p, c in zip(held_pieces, chips)]
    )
    home_far, home_far_sib = turn(
        [beyond] + [hop(beyond[i + 1], 0, c) for i, c in enumerate(chips)]
    )
    home = [home_near, home_far, hop(home_near_sib, 0, SIBLING), hop(home_far_sib, 0, SIBLING)]
    folds = [fold(home, cols, F32)[0] for cols in (first_cols, rest_cols)]
    total = jnp.concatenate(folds, axis=1) + jnp.concatenate(sent, axis=1).astype(F32)
    return grad_query[None], grad_kv[None], total


def shards(normed_input, queries, keys_values, grad_output, doc_lengths):
    ctx = lax.axis_size("ctx")
    own = lax.axis_index("ctx")
    shard_rows, model_width = normed_input.shape[1:]
    grad_query, lead, terms, held = attention(
        own[None], doc_lengths, queries[0], grad_output[0], keys_values[0], cube=False
    )
    span = terms.shape[0]
    moved = [shift(terms[span - 1 - d], -d) for d in range(1, span)]
    rest, grad_kv = settle(grad_query, lead, held, moved)
    grad_cols = jnp.concatenate([lead, rest], axis=1)
    part = model_width // ctx
    pieces = normed_input[0].reshape(shard_rows, ctx, part)
    my_features = lax.all_to_all(pieces, "ctx", split_axis=1, concat_axis=0, tiled=True)
    my_features = my_features.reshape(ctx * shard_rows, part)
    partial = fold_rows(my_features, lax.all_gather(grad_cols, "ctx", axis=0, tiled=True))
    grad_weights = lax.psum_scatter(
        partial.astype(BF16), "dp", scatter_dimension=0, tiled=True
    ).astype(F32)
    return grad_query[None], grad_kv[None], grad_weights


def solution(mesh):
    cube = mesh.shape["dp"] == 4 and mesh.shape["ctx"] == 8
    spec = P("dp", "ctx", None)
    return jax.shard_map(
        shards_cube if cube else shards,
        mesh=mesh,
        in_specs=(spec, spec, spec, spec, P("dp", None)),
        out_specs=(spec, spec, P(("ctx", "dp"), None)),
        check_vma=False,
    )
```
